32 devices in a mesh: row: 2 (over y), col: 16 (over z, x, core).
Axes of the slice: x: 2, y: 2, z: 4, core: 2. Of those that a mesh axis runs over, the one named last changes fastest.
Arguments:
- primal: float32 [16, 1024, 1024], P('col'), as said below
- dual_inv: float32 [16, 1024, 1024], P('col'), as said below
- col_values: bfloat16 [16, 16, 128, 4096], P(None, None, 'col'), as said below
- col_perm: int32 [16, 2048], replicated, may hold values from 0 to 2047, each once within a row
- slab_values: bfloat16 [16, 128, 4096], P('col', 'row'), as said below
- slab_tile: int32 [16, 128], P('col', 'row'), may hold values from 0 to 15
Outputs:
- schur_cyclic: float32 [128, 2048], P('row', 'col')
The draws below stay inside these ranges and needn't reach their ends.
Inputs may be any that keep to these rules, and one draw needn't show every extreme that they name: Each block's row of col_perm names every constraint exactly once. Each block of primal is symmetric. Each block of dual_inv is symmetric. `col_values`: every tile, read row-major as 64 x 64, is symmetric. `slab_values`: every tile, read row-major as 64 x 64, is symmetric.
All inputs are finite; a program needn't handle non-finite values.
Results may differ from the reference program's by a relative error of at most 0.0021.
Values may be sent and summed in bfloat16 or wider, within the bound.
A program may use at most 256 MiB of HBM per device.

```python
import jax
import jax.numpy as jnp
from jax import lax

NB = 1024
TILE = 64
TN = 16
S_DEV = 64
NBLK = 16
MT = 128
M = 2048
S = 128
RB = 32
N_ROW = 2


def draw_primal(key, part):
    key = jax.random.fold_in(key, 11)
    first, second = jax.random.split(key)
    noise = 0.05 * jax.random.normal(first, (NBLK, NB, NB), jnp.float32)
    noise = (noise + jnp.swapaxes(noise, 1, 2)) * 0.7071
    diagonal = jax.random.uniform(second, (NBLK, NB), jnp.float32, 3.0, 6.0)
    return noise + diagonal[:, :, None] * jnp.eye(NB, dtype=jnp.float32)


def draw_dual_inv(key, part):
    key = jax.random.fold_in(key, 23)
    first, second = jax.random.split(key)
    noise = 0.05 * jax.random.normal(first, (NBLK, NB, NB), jnp.float32)
    noise = (noise + jnp.swapaxes(noise, 1, 2)) * 0.7071
    diagonal = jax.random.uniform(second, (NBLK, NB), jnp.float32, 3.0, 6.0)
    return noise + diagonal[:, :, None] * jnp.eye(NB, dtype=jnp.float32)


def draw_col_values(key, part):
    key = jax.random.fold_in(key, 37)
    noise = 0.03 * jax.random.normal(key, (NBLK, TN, MT, TILE, TILE), jnp.float32)
    square = (noise + jnp.swapaxes(noise, 3, 4)) * 0.7071
    return square.reshape(NBLK, TN, MT, TILE * TILE).astype(jnp.bfloat16)


def draw_slab_values(key, part):
    key = jax.random.fold_in(key, 41)
    noise = 0.03 * jax.random.normal(key, (NBLK, S, TILE, TILE), jnp.float32)
    square = (noise + jnp.swapaxes(noise, 2, 3)) * 0.7071
    return square.reshape(NBLK, S, TILE * TILE).astype(jnp.bfloat16)


def touch_ends(array, key, smallest, largest):
    shape = array.shape
    place = [jax.random.randint(jax.random.fold_in(key, axis), (), 0, shape[axis]) for axis in range(len(shape))]
    array = array.at[tuple(place)].set(smallest)
    longest = shape.index(max(shape))
    place[longest] = (place[longest] + 1) % shape[longest]
    return array.at[tuple(place)].set(largest)


def setup_inputs(seed: int = 0) -> dict:
    key_of = jax.random.split(jax.random.key(seed), 7)
    primal = draw_primal(jax.random.fold_in(key_of[6], 71), 0)
    dual_inv = draw_dual_inv(jax.random.fold_in(key_of[6], 71), 0)
    col_values = draw_col_values(jax.random.fold_in(key_of[6], 71), 0)
    col_perm = jax.vmap(lambda own: jax.random.permutation(own, M))(jax.random.split(key_of[3], NBLK)).reshape((NBLK, M)).astype(jnp.int32)
    slab_values = draw_slab_values(jax.random.fold_in(key_of[6], 71), 0)
    slab_tile = touch_ends(jax.random.randint(key_of[5], (NBLK, S), 0, TN), jax.random.fold_in(key_of[5], 1), 0, TN - 1).astype(jnp.int32)
    return dict(primal=primal, dual_inv=dual_inv, col_values=col_values, col_perm=col_perm, slab_values=slab_values, slab_tile=slab_tile)


HIGHEST = lax.Precision.HIGHEST


def block_terms(primal_block, dual_block, slab_block, tiles_block):
    order = primal_block.shape[0]
    tile_size = order // (order // TILE)
    tile_count = order // tile_size
    slab_square = slab_block.reshape(-1, tile_size, tile_size)
    primal_rows = jnp.take(primal_block.reshape(tile_count, tile_size, order), tiles_block, axis=0)
    dual_rows = jnp.take(dual_block.reshape(tile_count, tile_size, order), tiles_block, axis=0)
    panel = jnp.einsum("sac,scn->san", slab_square.astype(jnp.float32), dual_rows, precision=HIGHEST)
    primal_split = primal_rows.reshape(-1, tile_size, tile_count, tile_size)
    panel_split = panel.reshape(-1, tile_size, tile_count, tile_size)
    terms = jnp.einsum("scue,scuf->suef", primal_split, panel_split, precision=HIGHEST)
    return terms.reshape(terms.shape[0], tile_count, tile_size * tile_size).astype(jnp.bfloat16)


def reference(primal, dual_inv, col_values, col_perm, slab_values, slab_tile):
    def step(total, index):
        terms = block_terms(primal[index], dual_inv[index], slab_values[index], slab_tile[index])
        contrib = jnp.einsum("sup,ukp->suk", terms.astype(jnp.float32), col_values[index].astype(jnp.float32), precision=HIGHEST)
        flat = contrib.reshape(contrib.shape[0], -1)
        placed = jnp.zeros_like(total).at[:, col_perm[index]].set(flat)
        return total + placed, None

    start_total = jnp.zeros((slab_values.shape[1], col_perm.shape[1]), jnp.float32)
    total, unused = lax.scan(step, start_total, jnp.arange(NBLK))
    blocked = total.reshape(S_DEV // RB, N_ROW, RB, total.shape[1])
    return jnp.transpose(blocked, (1, 0, 2, 3)).reshape(total.shape[0], total.shape[1])
```

```python
import jax
import jax.numpy as jnp
from jax import lax
from jax.sharding import PartitionSpec as P

TILE = 64
RB = 32


HIGHEST = lax.Precision.HIGHEST


def body(n_row, primal, dual_inv, col_values, col_perm, slab_values, slab_tile):
    tile_size = TILE
    tile_count = col_values.shape[1]
    order = primal.shape[1]
    columns = col_perm.shape[1]
    block = lax.axis_index("col")
    own = lax.axis_index("row")
    part = tile_count // n_row
    width = part * tile_size
    slab = lax.all_gather(slab_values[0], "row", axis=0, tiled=True)
    tiles = lax.all_gather(slab_tile[0], "row", axis=0, tiled=True)
    slab_rows = slab.shape[0]
    mine = lax.dynamic_slice_in_dim(col_values, own * part, part, axis=1)
    arrived = lax.all_to_all(mine, "col", split_axis=0, concat_axis=2, tiled=True)
    primal_cols = lax.dynamic_slice_in_dim(primal[0], own * width, width, axis=1)
    dual_cols = lax.dynamic_slice_in_dim(dual_inv[0], own * width, width, axis=1)
    slab_square = slab.reshape(slab_rows, tile_size, tile_size)
    primal_rows = jnp.take(primal_cols.reshape(tile_count, tile_size, width), tiles, axis=0)
    dual_rows = jnp.take(dual_cols.reshape(tile_count, tile_size, width), tiles, axis=0)
    panel = jnp.einsum(
        "sac,scn->san", slab_square.astype(jnp.float32), dual_rows, precision=HIGHEST
    )
    primal_split = primal_rows.reshape(slab_rows, tile_size, part, tile_size)
    panel_split = panel.reshape(slab_rows, tile_size, part, tile_size)
    terms = jnp.einsum("scue,scuf->suef", primal_split, panel_split, precision=HIGHEST)
    terms = terms.reshape(slab_rows, part, tile_size * tile_size).astype(jnp.bfloat16)
    contrib = jnp.einsum("sup,ukp->suk", terms, arrived[0], preferred_element_type=jnp.float32)
    contrib = contrib.reshape(slab_rows // (RB * n_row), n_row, RB, columns // n_row)
    contrib = jnp.transpose(contrib, (1, 0, 2, 3)).reshape(slab_rows, columns // n_row)
    contrib = lax.all_to_all(contrib, "row", split_axis=0, concat_axis=1, tiled=True)
    ordering = lax.dynamic_index_in_dim(col_perm, block, 0, keepdims=False)
    onehot = (ordering[:, None] == jnp.arange(columns)[None, :]).astype(jnp.float32)
    placed = jnp.dot(contrib, onehot, precision=HIGHEST)
    return lax.psum_scatter(placed, "col", scatter_dimension=1, tiled=True)


def solution(mesh):
    def run(*args):
        return body(mesh.shape["row"], *args)

    return jax.shard_map(
        run,
        mesh=mesh,
        in_specs=(
            P("col", None, None),
            P("col", None, None),
            P(None, None, "col", None),
            P(),
            P("col", "row", None),
            P("col", "row"),
        ),
        out_specs=P("row", "col"),
        check_vma=False,
    )
```

```python
import functools

import jax
import jax.numpy as jnp
from jax import lax
from jax.experimental import pallas as pl
from jax.experimental.pallas import tpu as pltpu
from jax.sharding import PartitionSpec as P

TILE = 64
HALF = TILE // 2
RB = 32
LANES = 128
GROUP = 16
ROLL = LANES - HALF
TOGETHER = 4
MESH = pl.DeviceIdType.MESH
NT = (((1,), (1,)), ((), ()))


def split(value):
    high = value.astype(jnp.bfloat16)
    low = (value - high.astype(jnp.float32)).astype(jnp.bfloat16)
    return high, low


def kernel(
    n_row, n_col, tiles_ref, x_ref, z_ref, s_ref, perm_ref, col_ref, out_ref,
    raw, send, recv, slab, folded, corner, left, mine, theirs, hot, placed, arrived,
    load_sem, c_send, c_recv, s_send, s_recv, y_send, y_recv, p_send, p_recv,
):
    me = lax.axis_index("col")
    own = lax.axis_index("row")
    s_dev = s_ref.shape[0]
    rows = n_row * s_dev
    groups = raw.shape[1]
    pairs = groups
    flat = groups * GROUP
    packed_tiles = TILE * TILE // 2 // LANES
    slots = perm_ref.shape[2]
    columns = hot.shape[1]

    barrier = pltpu.get_barrier_semaphore()
    for k in range(1, n_col):
        pl.semaphore_signal(barrier, inc=1, device_id={"col": lax.rem(me + k, n_col)}, device_id_type=MESH)
    for k in range(1, n_row):
        pl.semaphore_signal(barrier, inc=1, device_id={"row": lax.rem(own + k, n_row)}, device_id_type=MESH)
    pl.semaphore_wait(barrier, n_col + n_row - 2)

    def offset(n):
        return n_col // 2 + lax.div(n + 1, 2) * (1 - 2 * lax.rem(n, 2))

    def target(n):
        return lax.rem(me + offset(n), n_col)

    def load(n):
        slot = lax.rem(n, 2)
        return pltpu.make_async_copy(
            col_ref.at[target(n), pl.ds(own * groups, groups)], raw.at[slot], load_sem.at[slot]
        )

    def row_copy(src, dst, out_sem, in_sem, there, here):
        return pltpu.make_async_remote_copy(
            src_ref=src, dst_ref=dst.at[here], send_sem=out_sem.at[there], recv_sem=in_sem.at[here],
            device_id={"row": there}, device_id_type=MESH,
        )

    def c_copy(there, here):
        return pltpu.make_async_remote_copy(
            src_ref=send.at[there], dst_ref=recv.at[:, pl.ds(here * GROUP, GROUP)],
            send_sem=c_send.at[there], recv_sem=c_recv.at[here],
            device_id={"col": there}, device_id_type=MESH,
        )

    def p_copy(there, here):
        return pltpu.make_async_remote_copy(
            src_ref=placed.at[there], dst_ref=arrived.at[here],
            send_sem=p_send.at[there], recv_sem=p_recv.at[here],
            device_id={"col": there}, device_id_type=MESH,
        )

    for k in range(1, n_row):
        row_copy(s_ref, slab, s_send, s_recv, lax.rem(own + k, n_row), own).start()

    lane = lax.broadcasted_iota(jnp.int32, (flat, LANES), 1)
    odd = jnp.where(lane >= TILE, 1, 0)
    entry = lane - odd * TILE

    def pack(slot, store):
        rest = jnp.zeros((flat, LANES), jnp.float32)
        for j in range(packed_tiles):
            upper = raw[slot, :, :, j * LANES:(j + 1) * LANES].astype(jnp.float32).reshape(flat, LANES)
            start = (packed_tiles + j) * LANES
            lower = raw[slot, :, :, start:start + LANES].astype(jnp.float32).reshape(flat, LANES)
            row = odd + 2 * j
            both = jnp.where(entry >= row, upper, pltpu.roll(lower, ROLL, 1))
            store(j, both.astype(jnp.bfloat16).reshape(groups, GROUP, LANES))
            rest = jnp.where(entry == row + HALF, lower, rest)
        store(packed_tiles, rest.astype(jnp.bfloat16).reshape(groups, GROUP, LANES))

    load(0).start()

    def outgoing(n, carry):
        load(n + 1).start()
        load(n).wait()
        there = target(n)

        def store(j, value):
            send[there, :, :, j * LANES:(j + 1) * LANES] = value

        pack(lax.rem(n, 2), store)
        c_copy(there, me).start()
        return carry

    lax.fori_loop(0, n_col - 1, outgoing, 0)
    load(n_col - 1).wait()

    def keep(j, value):
        recv[:, pl.ds(pl.multiple_of(me * GROUP, GROUP), GROUP), j * LANES:(j + 1) * LANES] = value

    pack((n_col - 1) % 2, keep)

    slab[own] = s_ref[...]

    wide = lax.broadcasted_iota(jnp.int32, (TILE, LANES), 1)
    first = wide < TILE
    e = lax.broadcasted_iota(jnp.int32, (HALF, LANES), 0)
    f = lax.broadcasted_iota(jnp.int32, (HALF, LANES), 1)
    f = jnp.where(f >= TILE, f - TILE, f)

    def terms(n):
        there = lax.rem(own + lax.div(n, s_dev), n_row)
        inner = lax.rem(n, s_dev)
        i = there * s_dev + inner
        t = tiles_ref[i]
        panel = jnp.dot(slab[there, inner], z_ref[t], preferred_element_type=jnp.float32)
        high, low = split(panel)
        right = jnp.concatenate([high, low, high, low], axis=0)
        for v in range(pairs):
            cut = slice(v * LANES, (v + 1) * LANES)
            term = jnp.dot(x_ref[t, cut], right[:, cut], preferred_element_type=jnp.float32)
            term = term.astype(jnp.bfloat16).astype(jnp.float32)
            term = term + term.T
            term = jnp.where(first, term[:TILE], term[TILE:])
            upper, lower = term[:HALF], term[HALF:]
            both = jnp.where(f > e, upper, jnp.where(f < e, pltpu.roll(lower, ROLL, 1), 0.5 * upper))
            folded[pl.ds(pl.multiple_of((v * rows + i) * HALF, HALF), HALF), :] = both
            rest = jnp.sum(jnp.where(f == e + HALF, 0.5 * lower, 0.0), axis=0, keepdims=True)
            corner[pl.ds(v * rows + i, 1), :] = rest

    def several(n, carry):
        for k in range(TOGETHER):
            terms(n * TOGETHER + k)
        return carry

    lax.fori_loop(0, s_dev // TOGETHER, several, 0)
    for k in range(1, n_row):
        there = lax.rem(own + k, n_row)
        row_copy(s_ref, slab, s_send, s_recv, there, there).wait_recv()
    lax.fori_loop(s_dev // TOGETHER, rows // TOGETHER, several, 0)

    near = lax.broadcasted_iota(jnp.int32, (LANES, LANES), 1) < TILE
    chunks = rows // LANES

    def lay(n, carry):
        v = lax.div(n, chunks)
        chunk = lax.rem(n, chunks)
        base = (v * rows + chunk * LANES) * HALF
        for j in range(packed_tiles + 1):
            if j < packed_tiles:
                a = folded[pl.ds(base + 2 * j, LANES, stride=HALF), :]
                b = folded[pl.ds(base + 2 * j + 1, LANES, stride=HALF), :]
            else:
                a = b = corner[pl.ds(pl.multiple_of(v * rows + chunk * LANES, LANES), LANES), :]
            u0 = jnp.where(near, a, pltpu.roll(b, TILE, 1))
            u1 = jnp.where(near, pltpu.roll(a, TILE, 1), b)
            parts = split(u0) + split(u1)
            for k, value in enumerate(parts):
                at = pl.multiple_of(k * rows + chunk * LANES, LANES)
                left[v, pl.ds(at, LANES), j * LANES:(j + 1) * LANES] = value
        return carry

    lax.fori_loop(0, pairs * chunks, lay, 0)

    column = lax.broadcasted_iota(jnp.int32, (LANES, slots), 0)
    for r in range(n_row):

        def mark(n, carry):
            start = pl.multiple_of(n * LANES, LANES)
            value = jnp.where(column + n * LANES == perm_ref[r], 1.0, 0.0)
            hot[r, pl.ds(start, LANES), :] = value.astype(jnp.bfloat16)
            return carry

        lax.fori_loop(0, columns // LANES, mark, 0)

    def landed(n, carry):
        there = target(n)
        c_copy(there, there).wait_recv()
        return carry

    lax.fori_loop(0, n_col - 1, landed, 0)

    across = n_col * GROUP
    even = lax.rem(lax.broadcasted_iota(jnp.int32, (rows, across), 1), GROUP) < GROUP // 2
    for v in range(pairs):
        both = lax.dot_general(left[v], recv[v], NT, preferred_element_type=jnp.float32)
        u0 = both[:rows] + both[rows:2 * rows]
        u1 = both[2 * rows:3 * rows] + both[3 * rows:]
        value = jnp.where(even, u0, u1)
        for block in range(rows // RB):
            q, r = divmod(block, n_row)
            mine[r, q * RB:(q + 1) * RB, v * across:(v + 1) * across] = value[block * RB:(block + 1) * RB]

    for k in range(1, n_row):
        there = lax.rem(own + k, n_row)
        row_copy(mine.at[there], theirs, y_send, y_recv, there, own).start()
    theirs[own] = mine[own]

    def place(r, total):
        high, low = split(theirs[r])
        value = jnp.concatenate([high, low], axis=0)
        value = lax.dot_general(value, hot[r], NT, preferred_element_type=jnp.float32)
        value = value[:s_dev] + value[s_dev:]
        return value if total is None else total + value

    total = place(own, None)
    for k in range(1, n_row):
        there = lax.rem(own + k, n_row)
        row_copy(mine.at[there], theirs, y_send, y_recv, there, there).wait_recv()
        total = place(there, total)
    out_cols = columns // n_col
    for c in range(n_col):
        placed[c] = total[:, c * out_cols:(c + 1) * out_cols]

    def give(n, carry):
        p_copy(target(n), me).start()
        return carry

    lax.fori_loop(0, n_col - 1, give, 0)
    summed = placed[me]
    for k in range(1, n_col):
        there = lax.rem(me + k, n_col)
        p_copy(there, there).wait_recv()
        summed = summed + arrived[there]
    out_ref[...] = summed

    def done(n, carry):
        there = target(n)
        c_copy(there, me).wait_send()
        p_copy(there, me).wait_send()
        return carry

    lax.fori_loop(0, n_col - 1, done, 0)
    for k in range(1, n_row):
        there = lax.rem(own + k, n_row)
        row_copy(s_ref, slab, s_send, s_recv, there, own).wait_send()
        row_copy(mine.at[there], theirs, y_send, y_recv, there, own).wait_send()


def halves(value):
    high = lax.reduce_precision(value, 8, 7)
    low = value - high
    return high.astype(jnp.bfloat16), low.astype(jnp.bfloat16)


def body(n_row, n_col, primal, dual_inv, col_values, col_perm, slab_values, slab_tile):
    tile_count = col_values.shape[1]
    order = primal.shape[1]
    columns = col_perm.shape[1]
    s_dev = slab_values.shape[1]
    rows = n_row * s_dev
    keep = col_values.shape[2]
    block = lax.axis_index("col")
    own = lax.axis_index("row")
    part = tile_count // n_row
    width = part * TILE
    slots = columns // n_row
    tiles = lax.all_gather(slab_tile[0], "row", axis=0, tiled=True)

    x = lax.dynamic_slice_in_dim(primal[0], own * width, width, axis=0)
    x = jnp.transpose(x.reshape(width, order // TILE, TILE), (1, 0, 2))
    high, low = halves(x)
    x = jnp.concatenate([high, high, low, low], axis=2)
    z = lax.dynamic_slice_in_dim(dual_inv[0], own * width, width, axis=1)
    high, low = halves(z.reshape(order // TILE, TILE, width))
    z = jnp.concatenate([high, low], axis=1)
    s = slab_values[0].reshape(s_dev, TILE, TILE)
    s = jnp.concatenate([s, s], axis=2)
    perm = lax.dynamic_index_in_dim(col_perm, block, 0, keepdims=False)
    perm = perm.reshape(n_row, part // 2, 2, n_col, keep)
    perm = jnp.transpose(perm, (0, 1, 3, 2, 4)).reshape(n_row, 1, slots)
    col = col_values.reshape(n_col, tile_count * keep // GROUP, GROUP, TILE * TILE)

    groups = part * keep // GROUP
    packed = TILE * TILE // 2 + LANES
    vmem = pl.BlockSpec(memory_space=pltpu.VMEM)
    dma = pltpu.SemaphoreType.DMA
    f32, bf16 = jnp.float32, jnp.bfloat16
    return pl.pallas_call(
        functools.partial(kernel, n_row, n_col),
        out_shape=jax.ShapeDtypeStruct((s_dev, columns // n_col), f32),
        in_specs=[
            pl.BlockSpec(memory_space=pltpu.SMEM), vmem, vmem, vmem, vmem,
            pl.BlockSpec(memory_space=pl.ANY),
        ],
        out_specs=vmem,
        scratch_shapes=[
            pltpu.VMEM((2, groups, GROUP, TILE * TILE), bf16),
            pltpu.VMEM((n_col, groups, GROUP, packed), bf16),
            pltpu.VMEM((groups, n_col * GROUP, packed), bf16),
            pltpu.VMEM((n_row, s_dev, TILE, 2 * TILE), bf16),
            pltpu.VMEM((groups * rows * HALF, LANES), f32),
            pltpu.VMEM((groups * rows, LANES), f32),
            pltpu.VMEM((groups, 4 * rows, packed), bf16),
            pltpu.VMEM((n_row, s_dev, slots), f32),
            pltpu.VMEM((n_row, s_dev, slots), f32),
            pltpu.VMEM((n_row, columns, slots), bf16),
            pltpu.VMEM((n_col, s_dev, columns // n_col), f32),
            pltpu.VMEM((n_col, s_dev, columns // n_col), f32),
            dma((2,)), dma((n_col,)), dma((n_col,)), dma((n_row,)), dma((n_row,)),
            dma((n_row,)), dma((n_row,)), dma((n_col,)), dma((n_col,)),
        ],
        compiler_params=pltpu.CompilerParams(
            collective_id=0, has_side_effects=True, vmem_limit_bytes=60 * 1024 * 1024
        ),
    )(tiles, x, z, s, perm, col)


def solution(mesh):
    def run(*args):
        return body(mesh.shape["row"], mesh.shape["col"], *args)

    return jax.shard_map(
        run,
        mesh=mesh,
        in_specs=(
            P("col", None, None),
            P("col", None, None),
            P(None, None, "col", None),
            P(),
            P("col", "row", None),
            P("col", "row"),
        ),
        out_specs=P("row", "col"),
        check_vma=False,
    )
```

```python
import functools

import jax
import jax.numpy as jnp
from jax import lax
from jax.experimental import pallas as pl
from jax.experimental.pallas import tpu as pltpu
from jax.sharding import PartitionSpec as P

TILE = 64
HALF = TILE // 2
RB = 32
LANES = 128
GROUP = 16
ROLL = LANES - HALF
TOGETHER = 4
MESH = pl.DeviceIdType.MESH
NT = (((1,), (1,)), ((), ()))


def split(value):
    high = value.astype(jnp.bfloat16)
    low = (value - high.astype(jnp.float32)).astype(jnp.bfloat16)
    return high, low


def kernel(
    n_row, n_col, own_tile, tile_ref, perm_ref, x_hbm, z_hbm, s_hbm, col_ref, out_ref,
    x_raw, z_raw, x_ref, z_ref, tile_out, tile_in, tile_all, s_raw, slab,
    raw, send, recv, folded, corner, left, mine, theirs, hot, total, placed, arrived,
    load_sem, in_sem, c_send, c_recv, s_send, s_recv, t_send, t_recv, y_send, y_recv, p_send, p_recv,
):
    me = lax.axis_index("col")
    own = lax.axis_index("row")
    s_dev = s_hbm.shape[1]
    rows = n_row * s_dev
    pairs = send.shape[1]
    width = pairs * LANES
    packed_tiles = TILE * TILE // 2 // LANES
    across = n_col * GROUP
    columns = hot.shape[2]

    x_copy = pltpu.make_async_copy(x_hbm.at[0, pl.ds(own * width, width)], x_raw, in_sem.at[0])
    z_copy = pltpu.make_async_copy(
        z_hbm.at[0, :, pl.ds(pl.multiple_of(own * width, LANES), width)], z_raw, in_sem.at[1]
    )
    s_copy = pltpu.make_async_copy(s_hbm.at[0], s_raw.at[own], in_sem.at[2])
    x_copy.start()
    z_copy.start()
    s_copy.start()

    def offset(n):
        return n_col // 2 + lax.div(n + 1, 2) * (1 - 2 * lax.rem(n, 2))

    def target(n):
        return lax.rem(me + offset(n), n_col)

    def load(n):
        slot = lax.rem(n, 2)
        return pltpu.make_async_copy(
            col_ref.at[target(lax.rem(n, n_col)), own * pairs + lax.div(n, n_col)],
            raw.at[slot], load_sem.at[slot],
        )

    load(0).start()

    barrier = pltpu.get_barrier_semaphore()
    for k in range(1, n_col):
        pl.semaphore_signal(barrier, inc=1, device_id={"col": lax.rem(me + k, n_col)}, device_id_type=MESH)
    for k in range(1, n_row):
        pl.semaphore_signal(barrier, inc=1, device_id={"row": lax.rem(own + k, n_row)}, device_id_type=MESH)

    tile_out[...] = jnp.zeros_like(tile_out)
    tile_out[0:1, 0:s_dev] = tile_ref[...]
    pl.semaphore_wait(barrier, n_col + n_row - 2)

    def row_copy(src, dst, out_sem, in_sem, there):
        return pltpu.make_async_remote_copy(
            src_ref=src, dst_ref=dst, send_sem=out_sem, recv_sem=in_sem,
            device_id={"row": there}, device_id_type=MESH,
        )

    def tile_copy(there, here):
        return row_copy(tile_out, tile_in.at[here], t_send.at[there], t_recv.at[here], there)

    def slab_copy(there, here):
        return row_copy(s_hbm.at[0], s_raw.at[here], s_send.at[there], s_recv.at[here], there)

    def y_copy(v, there, here):
        return row_copy(
            mine.at[v, there], theirs.at[v, here], y_send.at[v, there], y_recv.at[v, here], there
        )

    def c_copy(v, there, here):
        return pltpu.make_async_remote_copy(
            src_ref=send.at[there, v], dst_ref=recv.at[v, pl.ds(here * GROUP, GROUP)],
            send_sem=c_send.at[v, there], recv_sem=c_recv.at[v, here],
            device_id={"col": there}, device_id_type=MESH,
        )

    def p_copy(there, here):
        return pltpu.make_async_remote_copy(
            src_ref=placed.at[there], dst_ref=arrived.at[here],
            send_sem=p_send.at[there], recv_sem=p_recv.at[here],
            device_id={"col": there}, device_id_type=MESH,
        )

    mates = [lax.rem(own + k, n_row) for k in range(1, n_row)]
    for there in mates:
        tile_copy(there, own).start()
        slab_copy(there, own).start()

    lane = lax.broadcasted_iota(jnp.int32, (GROUP, LANES), 1)
    odd = jnp.where(lane >= TILE, 1, 0)
    entry = lane - odd * TILE

    def pack(slot, store):
        rest = jnp.zeros((GROUP, LANES), jnp.float32)
        for j in range(packed_tiles):
            upper = raw[slot, :, j * LANES:(j + 1) * LANES].astype(jnp.float32)
            start = (packed_tiles + j) * LANES
            lower = raw[slot, :, start:start + LANES].astype(jnp.float32)
            row = odd + 2 * j
            both = jnp.where(entry >= row, upper, pltpu.roll(lower, ROLL, 1))
            store(j, both.astype(jnp.bfloat16))
            rest = jnp.where(entry == row + HALF, lower, rest)
        store(packed_tiles, rest.astype(jnp.bfloat16))

    steps = pairs * n_col

    def outgoing(n, carry):
        @pl.when(n + 1 < steps)
        def _():
            load(n + 1).start()

        load(n).wait()
        v = lax.div(n, n_col)
        step = lax.rem(n, n_col)
        there = target(step)

        def store(j, value):
            send[there, v, :, j * LANES:(j + 1) * LANES] = value

        pack(lax.rem(n, 2), store)

        @pl.when(step < n_col - 1)
        def _():
            c_copy(v, there, me).start()

        return carry

    lax.fori_loop(0, steps, outgoing, 0)
    for v in range(pairs):
        recv[v, pl.ds(pl.multiple_of(me * GROUP, GROUP), GROUP), :] = send[me, v]

    half = lax.broadcasted_iota(jnp.int32, (width, LANES), 1) < TILE
    x_copy.wait()
    for j in range(x_raw.shape[1] // LANES):
        a = x_raw[:, j * LANES:(j + 1) * LANES]
        b = pltpu.roll(a, TILE, 1)
        for k, value in enumerate((jnp.where(half, a, b), jnp.where(half, b, a))):
            high, low = split(value)
            x_ref[2 * j + k, :, :LANES] = high
            x_ref[2 * j + k, :, LANES:] = low
    z_copy.wait()

    def parts_of(t, carry):
        high, low = split(z_raw[pl.ds(pl.multiple_of(t * TILE, TILE), TILE), :])
        z_ref[t, :TILE] = high
        z_ref[t, TILE:] = low
        return carry

    lax.fori_loop(0, z_ref.shape[0], parts_of, 0)

    slab_half = lax.broadcasted_iota(jnp.int32, (s_dev, LANES), 1) < TILE

    def expand(r):
        for j in range(TILE * TILE // LANES):
            a = s_raw[r, :, j * LANES:(j + 1) * LANES].astype(jnp.float32)
            b = pltpu.roll(a, TILE, 1)
            slab[pl.ds(r * s_dev * TILE + 2 * j, s_dev, stride=TILE), :] = jnp.where(slab_half, a, b)
            slab[pl.ds(r * s_dev * TILE + 2 * j + 1, s_dev, stride=TILE), :] = jnp.where(slab_half, b, a)

    s_copy.wait()
    expand(own)

    wide = lax.broadcasted_iota(jnp.int32, (TILE, LANES), 1)
    first = wide < TILE
    e = lax.broadcasted_iota(jnp.int32, (HALF, LANES), 0)
    f = lax.broadcasted_iota(jnp.int32, (HALF, LANES), 1)
    f = jnp.where(f >= TILE, f - TILE, f)

    def terms(i, t):
        square = slab[pl.ds(pl.multiple_of(i * TILE, TILE), TILE), :].astype(jnp.bfloat16)
        panel = jnp.dot(square, z_ref[t], preferred_element_type=jnp.float32)
        high, low = split(panel)
        right = jnp.concatenate([high, low, high, low], axis=0)
        for v in range(pairs):
            cut = slice(v * LANES, (v + 1) * LANES)
            term = jnp.dot(x_ref[t, cut], right[:, cut], preferred_element_type=jnp.float32)
            term = term.astype(jnp.bfloat16).astype(jnp.float32)
            term = term + term.T
            term = jnp.where(first, term[:TILE], term[TILE:])
            upper, lower = term[:HALF], term[HALF:]
            both = jnp.where(f > e, upper, jnp.where(f < e, pltpu.roll(lower, ROLL, 1), 0.5 * upper))
            folded[pl.ds(pl.multiple_of((v * rows + i) * HALF, HALF), HALF), :] = both
            rest = jnp.sum(jnp.where(f == e + HALF, 0.5 * lower, 0.0), axis=0, keepdims=True)
            corner[pl.ds(v * rows + i, 1), :] = rest

    def first_rows(n, carry):
        for k in range(TOGETHER):
            inner = n * TOGETHER + k
            terms(own * s_dev + inner, own_tile[0, inner])
        return carry

    lax.fori_loop(0, s_dev // TOGETHER, first_rows, 0)
    for there in mates:
        tile_copy(there, there).wait_recv()
        slab_copy(there, there).wait_recv()
        expand(there)
    tile_in[own] = tile_out[...]
    tile_move = pltpu.make_async_copy(tile_in, tile_all, in_sem.at[3])
    tile_move.start()
    tile_move.wait()

    def other_rows(n, carry):
        for k in range(TOGETHER):
            at = n * TOGETHER + k
            there = lax.rem(own + lax.div(at, s_dev), n_row)
            inner = lax.rem(at, s_dev)
            terms(there * s_dev + inner, tile_all[there, 0, inner])
        return carry

    lax.fori_loop(s_dev // TOGETHER, rows // TOGETHER, other_rows, 0)

    near = lax.broadcasted_iota(jnp.int32, (LANES, LANES), 1) < TILE
    chunks = rows // LANES

    def lay(n, carry):
        v = lax.div(n, chunks)
        chunk = lax.rem(n, chunks)
        base = (v * rows + chunk * LANES) * HALF
        for j in range(packed_tiles + 1):
            if j < packed_tiles:
                a = folded[pl.ds(base + 2 * j, LANES, stride=HALF), :]
                b = folded[pl.ds(base + 2 * j + 1, LANES, stride=HALF), :]
            else:
                a = b = corner[pl.ds(pl.multiple_of(v * rows + chunk * LANES, LANES), LANES), :]
            u0 = jnp.where(near, a, pltpu.roll(b, TILE, 1))
            u1 = jnp.where(near, pltpu.roll(a, TILE, 1), b)
            parts = split(u0) + split(u1)
            for k, value in enumerate(parts):
                at = pl.multiple_of(k * rows + chunk * LANES, LANES)
                left[v, pl.ds(at, LANES), j * LANES:(j + 1) * LANES] = value
        return carry

    lax.fori_loop(0, pairs * chunks, lay, 0)

    column = lax.broadcasted_iota(jnp.int32, (LANES, across), 0)
    for r in range(n_row):
        for v in range(pairs):

            def mark(n, carry):
                start = pl.multiple_of(n * LANES, LANES)
                value = jnp.where(column + n * LANES == perm_ref[r, v], 1.0, 0.0)
                hot[r, v, pl.ds(start, LANES), :] = value.astype(jnp.bfloat16)
                return carry

            lax.fori_loop(0, columns // LANES, mark, 0)

    even = lax.rem(lax.broadcasted_iota(jnp.int32, (rows, across), 1), GROUP) < GROUP // 2

    def place(v, r, fresh):
        high, low = split(theirs[v, r])
        value = jnp.concatenate([high, low], axis=0)
        value = lax.dot_general(value, hot[r, v], NT, preferred_element_type=jnp.float32)
        value = value[:s_dev] + value[s_dev:]
        total[...] = value if fresh else total[...] + value

    def place_mates(v):
        for there in mates:
            y_copy(v, there, there).wait_recv()
            place(v, there, False)

    for v in range(pairs):

        def landed(n, carry):
            there = target(n)
            c_copy(v, there, there).wait_recv()
            return carry

        lax.fori_loop(0, n_col - 1, landed, 0)
        both = lax.dot_general(left[v], recv[v], NT, preferred_element_type=jnp.float32)
        u0 = both[:rows] + both[rows:2 * rows]
        u1 = both[2 * rows:3 * rows] + both[3 * rows:]
        value = jnp.where(even, u0, u1)
        for block in range(rows // RB):
            q, r = divmod(block, n_row)
            mine[v, r, q * RB:(q + 1) * RB, :] = value[block * RB:(block + 1) * RB]
        for there in mates:
            y_copy(v, there, own).start()
        theirs[v, own] = mine[v, own]
        place(v, own, v == 0)
        if v > 0:
            place_mates(v - 1)
    place_mates(pairs - 1)

    out_cols = columns // n_col
    for c in range(n_col):
        placed[c] = total[:, c * out_cols:(c + 1) * out_cols]

    def give(n, carry):
        p_copy(target(n), me).start()
        return carry

    lax.fori_loop(0, n_col - 1, give, 0)
    summed = placed[me]
    for k in range(1, n_col):
        there = lax.rem(me + k, n_col)
        p_copy(there, there).wait_recv()
        summed = summed + arrived[there]
    out_ref[...] = summed

    def done(n, carry):
        there = target(n)
        for v in range(pairs):
            c_copy(v, there, me).wait_send()
        p_copy(there, me).wait_send()
        return carry

    lax.fori_loop(0, n_col - 1, done, 0)
    for there in mates:
        tile_copy(there, own).wait_send()
        slab_copy(there, own).wait_send()
        for v in range(pairs):
            y_copy(v, there, own).wait_send()


def body(n_row, n_col, primal, dual_inv, col_values, col_perm, slab_values, slab_tile):
    tile_count = col_values.shape[1]
    order = primal.shape[1]
    columns = col_perm.shape[1]
    s_dev = slab_values.shape[1]
    rows = n_row * s_dev
    keep = col_values.shape[2]
    block = lax.axis_index("col")
    part = tile_count // n_row
    width = part * TILE
    pairs = part // 2
    perm = lax.dynamic_index_in_dim(col_perm, block, 0, keepdims=False)
    perm = perm.reshape(n_row, pairs, 2, n_col, keep)
    perm = jnp.transpose(perm, (0, 1, 3, 2, 4)).reshape(n_row, pairs, 1, n_col * 2 * keep)
    col = col_values.reshape(n_col, tile_count // 2, GROUP, TILE * TILE)

    packed = TILE * TILE // 2 + LANES
    out_cols = columns // n_col
    across = n_col * GROUP
    vmem = pl.BlockSpec(memory_space=pltpu.VMEM)
    whole = pl.BlockSpec(memory_space=pl.ANY)
    dma = pltpu.SemaphoreType.DMA
    f32, bf16, i32 = jnp.float32, jnp.bfloat16, jnp.int32
    return pl.pallas_call(
        functools.partial(kernel, n_row, n_col),
        out_shape=jax.ShapeDtypeStruct((s_dev, out_cols), f32),
        in_specs=[pl.BlockSpec(memory_space=pltpu.SMEM), vmem, vmem, whole, whole, whole, whole],
        out_specs=vmem,
        scratch_shapes=[
            pltpu.VMEM((width, order), f32),
            pltpu.VMEM((order, width), f32),
            pltpu.VMEM((order // TILE, width, 2 * LANES), bf16),
            pltpu.VMEM((order // TILE, 2 * TILE, width), bf16),
            pltpu.VMEM((8, LANES), i32),
            pltpu.VMEM((n_row, 8, LANES), i32),
            pltpu.SMEM((n_row, 8, LANES), i32),
            pltpu.VMEM((n_row, s_dev, TILE * TILE), bf16),
            pltpu.VMEM((rows * TILE, LANES), f32),
            pltpu.VMEM((2, GROUP, TILE * TILE), bf16),
            pltpu.VMEM((n_col, pairs, GROUP, packed), bf16),
            pltpu.VMEM((pairs, across, packed), bf16),
            pltpu.VMEM((pairs * rows * HALF, LANES), f32),
            pltpu.VMEM((pairs * rows, LANES), f32),
            pltpu.VMEM((pairs, 4 * rows, packed), bf16),
            pltpu.VMEM((pairs, n_row, s_dev, across), f32),
            pltpu.VMEM((pairs, n_row, s_dev, across), f32),
            pltpu.VMEM((n_row, pairs, columns, across), bf16),
            pltpu.VMEM((s_dev, columns), f32),
            pltpu.VMEM((n_col, s_dev, out_cols), f32),
            pltpu.VMEM((n_col, s_dev, out_cols), f32),
            dma((2,)), dma((4,)), dma((pairs, n_col)), dma((pairs, n_col)),
            dma((n_row,)), dma((n_row,)), dma((n_row,)), dma((n_row,)),
            dma((pairs, n_row)), dma((pairs, n_row)), dma((n_col,)), dma((n_col,)),
        ],
        compiler_params=pltpu.CompilerParams(
            collective_id=0, has_side_effects=True, vmem_limit_bytes=60 * 1024 * 1024
        ),
    )(slab_tile, slab_tile, perm, primal, dual_inv, slab_values, col)


def solution(mesh):
    def run(*args):
        return body(mesh.shape["row"], mesh.shape["col"], *args)

    return jax.shard_map(
        run,
        mesh=mesh,
        in_specs=(
            P("col", None, None),
            P("col", None, None),
            P(None, None, "col", None),
            P(),
            P("col", "row", None),
            P("col", "row"),
        ),
        out_specs=P("row", "col"),
        check_vma=False,
    )
```

```python
import functools

import jax
import jax.numpy as jnp
from jax import lax
from jax.experimental import pallas as pl
from jax.experimental.pallas import tpu as pltpu
from jax.sharding import PartitionSpec as P

TILE = 64
HALF = TILE // 2
RB = 32
LANES = 128
GROUP = 16
ROLL = LANES - HALF
TOGETHER = 4
AHEAD = 16
MESH = pl.DeviceIdType.MESH
NT = (((1,), (1,)), ((), ()))


def split(value):
    high = value.astype(jnp.bfloat16)
    low = (value - high.astype(jnp.float32)).astype(jnp.bfloat16)
    return high, low


def kernel(
    n_row, n_col, own_tile, tile_ref, perm_ref, x_hbm, z_hbm, s_hbm, col_ref, out_ref,
    x_raw, z_raw, x_ref, z_ref, tile_out, tile_in, tile_all, s_raw, slab,
    raw, send, recv, folded, corner, left, mine, theirs, hot, total, placed, arrived,
    load_sem, in_sem, c_send, c_recv, s_send, s_recv, t_send, t_recv, y_send, y_recv, p_send, p_recv,
):
    me = lax.axis_index("col")
    own = lax.axis_index("row")
    s_dev = s_hbm.shape[1]
    rows = n_row * s_dev
    pairs = send.shape[1]
    width = pairs * LANES
    packed_tiles = TILE * TILE // 2 // LANES
    across = n_col * GROUP
    columns = hot.shape[2]

    x_copy = pltpu.make_async_copy(x_hbm.at[0, pl.ds(own * width, width)], x_raw, in_sem.at[0])
    z_copy = pltpu.make_async_copy(
        z_hbm.at[0, :, pl.ds(pl.multiple_of(own * width, LANES), width)], z_raw, in_sem.at[1]
    )
    s_copy = pltpu.make_async_copy(s_hbm.at[0], s_raw.at[own], in_sem.at[2])
    x_copy.start()
    z_copy.start()
    s_copy.start()

    def offset(n):
        return n_col // 2 + lax.div(n + 1, 2) * (1 - 2 * lax.rem(n, 2))

    def target(n):
        return lax.rem(me + offset(n), n_col)

    def load(n):
        slot = lax.rem(n, AHEAD)
        return pltpu.make_async_copy(
            col_ref.at[target(lax.rem(n, n_col)), own * pairs + lax.div(n, n_col)],
            raw.at[slot], load_sem.at[slot],
        )

    steps = pairs * n_col
    for n in range(min(AHEAD - 1, steps)):
        load(n).start()

    barrier = pltpu.get_barrier_semaphore()
    for k in range(1, n_col):
        pl.semaphore_signal(barrier, inc=1, device_id={"col": lax.rem(me + k, n_col)}, device_id_type=MESH)
    for k in range(1, n_row):
        pl.semaphore_signal(barrier, inc=1, device_id={"row": lax.rem(own + k, n_row)}, device_id_type=MESH)

    tile_out[...] = jnp.zeros_like(tile_out)
    tile_out[0:1, 0:s_dev] = tile_ref[...]
    pl.semaphore_wait(barrier, n_col + n_row - 2)

    def row_copy(src, dst, out_sem, in_sem, there):
        return pltpu.make_async_remote_copy(
            src_ref=src, dst_ref=dst, send_sem=out_sem, recv_sem=in_sem,
            device_id={"row": there}, device_id_type=MESH,
        )

    def tile_copy(there, here):
        return row_copy(tile_out, tile_in.at[here], t_send.at[there], t_recv.at[here], there)

    def slab_copy(there, here):
        return row_copy(s_hbm.at[0], s_raw.at[here], s_send.at[there], s_recv.at[here], there)

    def y_copy(v, there, here):
        return row_copy(
            mine.at[v, there], theirs.at[v, here], y_send.at[v, there], y_recv.at[v, here], there
        )

    def c_copy(v, there, here):
        return pltpu.make_async_remote_copy(
            src_ref=send.at[there, v], dst_ref=recv.at[v, pl.ds(here * GROUP, GROUP)],
            send_sem=c_send.at[v, there], recv_sem=c_recv.at[v, here],
            device_id={"col": there}, device_id_type=MESH,
        )

    def p_copy(there, here):
        return pltpu.make_async_remote_copy(
            src_ref=placed.at[there], dst_ref=arrived.at[here],
            send_sem=p_send.at[there], recv_sem=p_recv.at[here],
            device_id={"col": there}, device_id_type=MESH,
        )

    mates = [lax.rem(own + k, n_row) for k in range(1, n_row)]
    for there in mates:
        tile_copy(there, own).start()
        slab_copy(there, own).start()

    lane = lax.broadcasted_iota(jnp.int32, (GROUP, LANES), 1)
    odd = jnp.where(lane >= TILE, 1, 0)
    entry = lane - odd * TILE

    def pack(slot, store):
        rest = jnp.zeros((GROUP, LANES), jnp.float32)
        for j in range(packed_tiles):
            upper = raw[slot, :, j * LANES:(j + 1) * LANES].astype(jnp.float32)
            start = (packed_tiles + j) * LANES
            lower = raw[slot, :, start:start + LANES].astype(jnp.float32)
            row = odd + 2 * j
            both = jnp.where(entry >= row, upper, pltpu.roll(lower, ROLL, 1))
            store(j, both.astype(jnp.bfloat16))
            rest = jnp.where(entry == row + HALF, lower, rest)
        store(packed_tiles, rest.astype(jnp.bfloat16))

    def outgoing(n, carry):
        @pl.when(n + AHEAD - 1 < steps)
        def _():
            load(n + AHEAD - 1).start()

        load(n).wait()
        v = lax.div(n, n_col)
        step = lax.rem(n, n_col)
        there = target(step)

        def store(j, value):
            send[there, v, :, j * LANES:(j + 1) * LANES] = value

        pack(lax.rem(n, AHEAD), store)

        @pl.when(step < n_col - 1)
        def _():
            c_copy(v, there, me).start()

        return carry

    lax.fori_loop(0, steps, outgoing, 0)
    for v in range(pairs):
        recv[v, pl.ds(pl.multiple_of(me * GROUP, GROUP), GROUP), :] = send[me, v]

    half = lax.broadcasted_iota(jnp.int32, (width, LANES), 1) < TILE
    x_copy.wait()
    for j in range(x_raw.shape[1] // LANES):
        a = x_raw[:, j * LANES:(j + 1) * LANES]
        b = pltpu.roll(a, TILE, 1)
        for k, value in enumerate((jnp.where(half, a, b), jnp.where(half, b, a))):
            high, low = split(value)
            x_ref[2 * j + k, :, :LANES] = high
            x_ref[2 * j + k, :, LANES:] = low
    z_copy.wait()

    def parts_of(t, carry):
        high, low = split(z_raw[pl.ds(pl.multiple_of(t * TILE, TILE), TILE), :])
        z_ref[t, :TILE] = high
        z_ref[t, TILE:] = low
        return carry

    lax.fori_loop(0, z_ref.shape[0], parts_of, 0)

    slab_half = lax.broadcasted_iota(jnp.int32, (s_dev, LANES), 1) < TILE

    def expand(r):
        for j in range(TILE * TILE // LANES):
            a = s_raw[r, :, j * LANES:(j + 1) * LANES].astype(jnp.float32)
            b = pltpu.roll(a, TILE, 1)
            slab[pl.ds(r * s_dev * TILE + 2 * j, s_dev, stride=TILE), :] = jnp.where(slab_half, a, b)
            slab[pl.ds(r * s_dev * TILE + 2 * j + 1, s_dev, stride=TILE), :] = jnp.where(slab_half, b, a)

    s_copy.wait()
    expand(own)

    wide = lax.broadcasted_iota(jnp.int32, (TILE, LANES), 1)
    first = wide < TILE
    e = lax.broadcasted_iota(jnp.int32, (HALF, LANES), 0)
    f = lax.broadcasted_iota(jnp.int32, (HALF, LANES), 1)
    f = jnp.where(f >= TILE, f - TILE, f)

    def terms(i, t):
        square = slab[pl.ds(pl.multiple_of(i * TILE, TILE), TILE), :].astype(jnp.bfloat16)
        panel = jnp.dot(square, z_ref[t], preferred_element_type=jnp.float32)
        high, low = split(panel)
        right = jnp.concatenate([high, low, high, low], axis=0)
        done = []
        for v in range(pairs):
            cut = slice(v * LANES, (v + 1) * LANES)
            term = jnp.dot(x_ref[t, cut], right[:, cut], preferred_element_type=jnp.float32)
            term = jnp.where(first, term[:TILE], term[TILE:])
            done.append(term.astype(jnp.bfloat16).astype(jnp.float32))
        if pairs % 2:
            done.append(done[-1])
        for v in range(0, len(done), 2):
            turned = jnp.concatenate(done[v:v + 2], axis=0).T
            crossed = pltpu.roll(turned, TILE, 1)
            done[v] += jnp.where(first, turned[:TILE], crossed[TILE:])
            done[v + 1] += jnp.where(first, crossed[:TILE], turned[TILE:])
        for v in range(pairs):
            upper, lower = done[v][:HALF], done[v][HALF:]
            both = jnp.where(f > e, upper, jnp.where(f < e, pltpu.roll(lower, ROLL, 1), 0.5 * upper))
            folded[pl.ds(pl.multiple_of((v * rows + i) * HALF, HALF), HALF), :] = both
            rest = jnp.sum(jnp.where(f == e + HALF, 0.5 * lower, 0.0), axis=0, keepdims=True)
            corner[pl.ds(v * rows + i, 1), :] = rest

    def first_rows(n, carry):
        for k in range(TOGETHER):
            inner = n * TOGETHER + k
            terms(own * s_dev + inner, own_tile[0, inner])
        return carry

    lax.fori_loop(0, s_dev // TOGETHER, first_rows, 0)
    for there in mates:
        tile_copy(there, there).wait_recv()
        slab_copy(there, there).wait_recv()
        expand(there)
    tile_in[own] = tile_out[...]
    tile_move = pltpu.make_async_copy(tile_in, tile_all, in_sem.at[3])
    tile_move.start()
    tile_move.wait()

    def other_rows(n, carry):
        for k in range(TOGETHER):
            at = n * TOGETHER + k
            there = lax.rem(own + lax.div(at, s_dev), n_row)
            inner = lax.rem(at, s_dev)
            terms(there * s_dev + inner, tile_all[there, 0, inner])
        return carry

    lax.fori_loop(s_dev // TOGETHER, rows // TOGETHER, other_rows, 0)

    near = lax.broadcasted_iota(jnp.int32, (LANES, LANES), 1) < TILE
    chunks = rows // LANES

    def lay(n, carry):
        v = lax.div(n, chunks)
        chunk = lax.rem(n, chunks)
        base = (v * rows + chunk * LANES) * HALF
        for j in range(packed_tiles + 1):
            if j < packed_tiles:
                a = folded[pl.ds(base + 2 * j, LANES, stride=HALF), :]
                b = folded[pl.ds(base + 2 * j + 1, LANES, stride=HALF), :]
            else:
                a = b = corner[pl.ds(pl.multiple_of(v * rows + chunk * LANES, LANES), LANES), :]
            u0 = jnp.where(near, a, pltpu.roll(b, TILE, 1))
            u1 = jnp.where(near, pltpu.roll(a, TILE, 1), b)
            parts = split(u0) + split(u1)
            for k, value in enumerate(parts):
                at = pl.multiple_of(k * rows + chunk * LANES, LANES)
                left[v, pl.ds(at, LANES), j * LANES:(j + 1) * LANES] = value
        return carry

    lax.fori_loop(0, pairs * chunks, lay, 0)

    column = lax.broadcasted_iota(jnp.int32, (LANES, across), 0)
    for r in range(n_row):
        for v in range(pairs):

            def mark(n, carry):
                start = pl.multiple_of(n * LANES, LANES)
                value = jnp.where(column + n * LANES == perm_ref[r, v], 1.0, 0.0)
                hot[r, v, pl.ds(start, LANES), :] = value.astype(jnp.bfloat16)
                return carry

            lax.fori_loop(0, columns // LANES, mark, 0)

    even = lax.rem(lax.broadcasted_iota(jnp.int32, (rows, across), 1), GROUP) < GROUP // 2

    def place(v, r, fresh):
        high, low = split(theirs[v, r])
        value = jnp.concatenate([high, low], axis=0)
        value = lax.dot_general(value, hot[r, v], NT, preferred_element_type=jnp.float32)
        value = value[:s_dev] + value[s_dev:]
        total[...] = value if fresh else total[...] + value

    def place_mates(v):
        for there in mates:
            y_copy(v, there, there).wait_recv()
            place(v, there, False)

    for v in range(pairs):

        def landed(n, carry):
            there = target(n)
            c_copy(v, there, there).wait_recv()
            return carry

        lax.fori_loop(0, n_col - 1, landed, 0)
        both = lax.dot_general(left[v], recv[v], NT, preferred_element_type=jnp.float32)
        u0 = both[:rows] + both[rows:2 * rows]
        u1 = both[2 * rows:3 * rows] + both[3 * rows:]
        value = jnp.where(even, u0, u1)
        for block in range(rows // RB):
            q, r = divmod(block, n_row)
            mine[v, r, q * RB:(q + 1) * RB, :] = value[block * RB:(block + 1) * RB]
        for there in mates:
            y_copy(v, there, own).start()
        theirs[v, own] = mine[v, own]
        place(v, own, v == 0)
        if v > 0:
            place_mates(v - 1)
    place_mates(pairs - 1)

    out_cols = columns // n_col
    for c in range(n_col):
        placed[c] = total[:, c * out_cols:(c + 1) * out_cols]

    def give(n, carry):
        p_copy(target(n), me).start()
        return carry

    lax.fori_loop(0, n_col - 1, give, 0)
    summed = placed[me]
    for k in range(1, n_col):
        there = lax.rem(me + k, n_col)
        p_copy(there, there).wait_recv()
        summed = summed + arrived[there]
    out_ref[...] = summed

    def done(n, carry):
        there = target(n)
        for v in range(pairs):
            c_copy(v, there, me).wait_send()
        p_copy(there, me).wait_send()
        return carry

    lax.fori_loop(0, n_col - 1, done, 0)
    for there in mates:
        tile_copy(there, own).wait_send()
        slab_copy(there, own).wait_send()
        for v in range(pairs):
            y_copy(v, there, own).wait_send()


def body(n_row, n_col, primal, dual_inv, col_values, col_perm, slab_values, slab_tile):
    tile_count = col_values.shape[1]
    order = primal.shape[1]
    columns = col_perm.shape[1]
    s_dev = slab_values.shape[1]
    rows = n_row * s_dev
    keep = col_values.shape[2]
    block = lax.axis_index("col")
    part = tile_count // n_row
    width = part * TILE
    pairs = part // 2
    perm = lax.dynamic_index_in_dim(col_perm, block, 0, keepdims=False)
    perm = perm.reshape(n_row, pairs, 2, n_col, keep)
    perm = jnp.transpose(perm, (0, 1, 3, 2, 4)).reshape(n_row, pairs, 1, n_col * 2 * keep)
    col = col_values.reshape(n_col, tile_count // 2, GROUP, TILE * TILE)

    packed = TILE * TILE // 2 + LANES
    out_cols = columns // n_col
    across = n_col * GROUP
    vmem = pl.BlockSpec(memory_space=pltpu.VMEM)
    whole = pl.BlockSpec(memory_space=pl.ANY)
    dma = pltpu.SemaphoreType.DMA
    f32, bf16, i32 = jnp.float32, jnp.bfloat16, jnp.int32
    return pl.pallas_call(
        functools.partial(kernel, n_row, n_col),
        out_shape=jax.ShapeDtypeStruct((s_dev, out_cols), f32),
        in_specs=[pl.BlockSpec(memory_space=pltpu.SMEM), vmem, vmem, whole, whole, whole, whole],
        out_specs=vmem,
        scratch_shapes=[
            pltpu.VMEM((width, order), f32),
            pltpu.VMEM((order, width), f32),
            pltpu.VMEM((order // TILE, width, 2 * LANES), bf16),
            pltpu.VMEM((order // TILE, 2 * TILE, width), bf16),
            pltpu.VMEM((8, LANES), i32),
            pltpu.VMEM((n_row, 8, LANES), i32),
            pltpu.SMEM((n_row, 8, LANES), i32),
            pltpu.VMEM((n_row, s_dev, TILE * TILE), bf16),
            pltpu.VMEM((rows * TILE, LANES), f32),
            pltpu.VMEM((AHEAD, GROUP, TILE * TILE), bf16),
            pltpu.VMEM((n_col, pairs, GROUP, packed), bf16),
            pltpu.VMEM((pairs, across, packed), bf16),
            pltpu.VMEM((pairs * rows * HALF, LANES), f32),
            pltpu.VMEM((pairs * rows, LANES), f32),
            pltpu.VMEM((pairs, 4 * rows, packed), bf16),
            pltpu.VMEM((pairs, n_row, s_dev, across), f32),
            pltpu.VMEM((pairs, n_row, s_dev, across), f32),
            pltpu.VMEM((n_row, pairs, columns, across), bf16),
            pltpu.VMEM((s_dev, columns), f32),
            pltpu.VMEM((n_col, s_dev, out_cols), f32),
            pltpu.VMEM((n_col, s_dev, out_cols), f32),
            dma((AHEAD,)), dma((4,)), dma((pairs, n_col)), dma((pairs, n_col)),
            dma((n_row,)), dma((n_row,)), dma((n_row,)), dma((n_row,)),
            dma((pairs, n_row)), dma((pairs, n_row)), dma((n_col,)), dma((n_col,)),
        ],
        compiler_params=pltpu.CompilerParams(
            collective_id=0, has_side_effects=True, vmem_limit_bytes=60 * 1024 * 1024
        ),
    )(slab_tile, slab_tile, perm, primal, dual_inv, slab_values, col)


def solution(mesh):
    def run(*args):
        return body(mesh.shape["row"], mesh.shape["col"], *args)

    return jax.shard_map(
        run,
        mesh=mesh,
        in_specs=(
            P("col", None, None),
            P("col", None, None),
            P(None, None, "col", None),
            P(),
            P("col", "row", None),
            P("col", "row"),
        ),
        out_specs=P("row", "col"),
        check_vma=False,
    )
```

```python
import functools

import jax
import jax.numpy as jnp
from jax import lax
from jax.experimental import pallas as pl
from jax.experimental.pallas import tpu as pltpu
from jax.sharding import PartitionSpec as P

TILE = 64
HALF = TILE // 2
RB = 32
LANES = 128
GROUP = 16
ROLL = LANES - HALF
TOGETHER = 4
AHEAD = 16
MESH = pl.DeviceIdType.MESH
NT = (((1,), (1,)), ((), ()))


def split(value):
    high = value.astype(jnp.bfloat16)
    low = (value - high.astype(jnp.float32)).astype(jnp.bfloat16)
    return high, low


def kernel(
    n_row, n_col, own_tile, tile_ref, perm_ref, x_hbm, z_hbm, s_hbm, col_ref, out_ref,
    x_raw, z_raw, x_ref, z_ref, tile_out, tile_in, tile_all, s_raw, slab,
    raw, send, recv, folded, corner, left, mine, theirs, hot, total, placed, arrived,
    load_sem, in_sem, c_send, c_recv, s_send, s_recv, t_send, t_recv, y_send, y_recv, p_send, p_recv,
):
    me = lax.axis_index("col")
    own = lax.axis_index("row")
    s_dev = s_hbm.shape[1]
    rows = n_row * s_dev
    pairs = send.shape[1]
    width = pairs * LANES
    packed_tiles = TILE * TILE // 2 // LANES
    across = n_col * GROUP
    columns = hot.shape[2]

    x_copy = pltpu.make_async_copy(x_hbm.at[0, pl.ds(own * width, width)], x_raw, in_sem.at[0])
    z_copy = pltpu.make_async_copy(
        z_hbm.at[0, :, pl.ds(pl.multiple_of(own * width, LANES), width)], z_raw, in_sem.at[1]
    )
    s_copy = pltpu.make_async_copy(s_hbm.at[0], s_raw.at[own], in_sem.at[2])
    x_copy.start()
    z_copy.start()
    s_copy.start()

    half_col = n_col // 2
    my_half = lax.div(me, half_col)
    my_place = lax.rem(me, half_col)

    def target(n):
        near = lax.rem(n, 2)
        side = near * my_half + (1 - near) * (1 - my_half)
        return side * half_col + lax.rem(my_place + lax.div(n + 1, 2), half_col)

    def load(n):
        slot = lax.rem(n, AHEAD)
        return pltpu.make_async_copy(
            col_ref.at[target(lax.rem(n, n_col)), own * pairs + lax.div(n, n_col)],
            raw.at[slot], load_sem.at[slot],
        )

    steps = pairs * n_col
    for n in range(min(AHEAD - 1, steps)):
        load(n).start()

    barrier = pltpu.get_barrier_semaphore()
    for k in range(1, n_col):
        pl.semaphore_signal(barrier, inc=1, device_id={"col": lax.rem(me + k, n_col)}, device_id_type=MESH)
    for k in range(1, n_row):
        pl.semaphore_signal(barrier, inc=1, device_id={"row": lax.rem(own + k, n_row)}, device_id_type=MESH)

    tile_out[...] = jnp.zeros_like(tile_out)
    tile_out[0:1, 0:s_dev] = tile_ref[...]
    pl.semaphore_wait(barrier, n_col + n_row - 2)

    def row_copy(src, dst, out_sem, in_sem, there):
        return pltpu.make_async_remote_copy(
            src_ref=src, dst_ref=dst, send_sem=out_sem, recv_sem=in_sem,
            device_id={"row": there}, device_id_type=MESH,
        )

    def tile_copy(there, here):
        return row_copy(tile_out, tile_in.at[here], t_send.at[there], t_recv.at[here], there)

    def slab_copy(there, here):
        return row_copy(s_hbm.at[0], s_raw.at[here], s_send.at[there], s_recv.at[here], there)

    def y_copy(v, there, here):
        return row_copy(
            mine.at[v, there], theirs.at[v, here], y_send.at[v, there], y_recv.at[v, here], there
        )

    def c_copy(v, there, here):
        return pltpu.make_async_remote_copy(
            src_ref=send.at[there, v], dst_ref=recv.at[v, pl.ds(here * GROUP, GROUP)],
            send_sem=c_send.at[v, there], recv_sem=c_recv.at[v, here],
            device_id={"col": there}, device_id_type=MESH,
        )

    def p_copy(there, here):
        return pltpu.make_async_remote_copy(
            src_ref=placed.at[there], dst_ref=arrived.at[here],
            send_sem=p_send.at[there], recv_sem=p_recv.at[here],
            device_id={"col": there}, device_id_type=MESH,
        )

    mates = [lax.rem(own + k, n_row) for k in range(1, n_row)]
    for there in mates:
        tile_copy(there, own).start()
        slab_copy(there, own).start()

    lane = lax.broadcasted_iota(jnp.int32, (GROUP, LANES), 1)
    odd = jnp.where(lane >= TILE, 1, 0)
    entry = lane - odd * TILE

    def pack(slot, store):
        rest = jnp.zeros((GROUP, LANES), jnp.float32)
        for j in range(packed_tiles):
            upper = raw[slot, :, j * LANES:(j + 1) * LANES].astype(jnp.float32)
            start = (packed_tiles + j) * LANES
            lower = raw[slot, :, start:start + LANES].astype(jnp.float32)
            row = odd + 2 * j
            both = jnp.where(entry >= row, upper, pltpu.roll(lower, ROLL, 1))
            store(j, both.astype(jnp.bfloat16))
            rest = jnp.where(entry == row + HALF, lower, rest)
        store(packed_tiles, rest.astype(jnp.bfloat16))

    def outgoing(n, carry):
        @pl.when(n + AHEAD - 1 < steps)
        def _():
            load(n + AHEAD - 1).start()

        load(n).wait()
        v = lax.div(n, n_col)
        step = lax.rem(n, n_col)
        there = target(step)

        def store(j, value):
            send[there, v, :, j * LANES:(j + 1) * LANES] = value

        pack(lax.rem(n, AHEAD), store)

        @pl.when(step < n_col - 1)
        def _():
            c_copy(v, there, me).start()

        return carry

    lax.fori_loop(0, steps, outgoing, 0)
    for v in range(pairs):
        recv[v, pl.ds(pl.multiple_of(me * GROUP, GROUP), GROUP), :] = send[me, v]

    half = lax.broadcasted_iota(jnp.int32, (width, LANES), 1) < TILE
    x_copy.wait()
    for j in range(x_raw.shape[1] // LANES):
        a = x_raw[:, j * LANES:(j + 1) * LANES]
        b = pltpu.roll(a, TILE, 1)
        for k, value in enumerate((jnp.where(half, a, b), jnp.where(half, b, a))):
            high, low = split(value)
            x_ref[2 * j + k, :, :LANES] = high
            x_ref[2 * j + k, :, LANES:] = low
    z_copy.wait()

    def parts_of(t, carry):
        high, low = split(z_raw[pl.ds(pl.multiple_of(t * TILE, TILE), TILE), :])
        z_ref[t, :TILE] = high
        z_ref[t, TILE:] = low
        return carry

    lax.fori_loop(0, z_ref.shape[0], parts_of, 0)

    slab_half = lax.broadcasted_iota(jnp.int32, (s_dev, LANES), 1) < TILE

    def expand(r):
        for j in range(TILE * TILE // LANES):
            a = s_raw[r, :, j * LANES:(j + 1) * LANES].astype(jnp.float32)
            b = pltpu.roll(a, TILE, 1)
            slab[pl.ds(r * s_dev * TILE + 2 * j, s_dev, stride=TILE), :] = jnp.where(slab_half, a, b)
            slab[pl.ds(r * s_dev * TILE + 2 * j + 1, s_dev, stride=TILE), :] = jnp.where(slab_half, b, a)

    s_copy.wait()
    expand(own)

    wide = lax.broadcasted_iota(jnp.int32, (TILE, LANES), 1)
    first = wide < TILE
    e = lax.broadcasted_iota(jnp.int32, (HALF, LANES), 0)
    f = lax.broadcasted_iota(jnp.int32, (HALF, LANES), 1)
    f = jnp.where(f >= TILE, f - TILE, f)

    def terms(i, t):
        square = slab[pl.ds(pl.multiple_of(i * TILE, TILE), TILE), :].astype(jnp.bfloat16)
        panel = jnp.dot(square, z_ref[t], preferred_element_type=jnp.float32)
        high, low = split(panel)
        right = jnp.concatenate([high, low, high, low], axis=0)
        done = []
        for v in range(pairs):
            cut = slice(v * LANES, (v + 1) * LANES)
            term = jnp.dot(x_ref[t, cut], right[:, cut], preferred_element_type=jnp.float32)
            term = jnp.where(first, term[:TILE], term[TILE:])
            done.append(term.astype(jnp.bfloat16).astype(jnp.float32))
        if pairs % 2:
            done.append(done[-1])
        for v in range(0, len(done), 2):
            turned = jnp.concatenate(done[v:v + 2], axis=0).T
            crossed = pltpu.roll(turned, TILE, 1)
            done[v] += jnp.where(first, turned[:TILE], crossed[TILE:])
            done[v + 1] += jnp.where(first, crossed[:TILE], turned[TILE:])
        for v in range(pairs):
            upper, lower = done[v][:HALF], done[v][HALF:]
            both = jnp.where(f > e, upper, jnp.where(f < e, pltpu.roll(lower, ROLL, 1), 0.5 * upper))
            folded[pl.ds(pl.multiple_of((v * rows + i) * HALF, HALF), HALF), :] = both
            rest = jnp.sum(jnp.where(f == e + HALF, 0.5 * lower, 0.0), axis=0, keepdims=True)
            corner[pl.ds(v * rows + i, 1), :] = rest

    def first_rows(n, carry):
        for k in range(TOGETHER):
            inner = n * TOGETHER + k
            terms(own * s_dev + inner, own_tile[0, inner])
        return carry

    lax.fori_loop(0, s_dev // TOGETHER, first_rows, 0)
    for there in mates:
        tile_copy(there, there).wait_recv()
        slab_copy(there, there).wait_recv()
        expand(there)
    tile_in[own] = tile_out[...]
    tile_move = pltpu.make_async_copy(tile_in, tile_all, in_sem.at[3])
    tile_move.start()
    tile_move.wait()

    def other_rows(n, carry):
        for k in range(TOGETHER):
            at = n * TOGETHER + k
            there = lax.rem(own + lax.div(at, s_dev), n_row)
            inner = lax.rem(at, s_dev)
            terms(there * s_dev + inner, tile_all[there, 0, inner])
        return carry

    lax.fori_loop(s_dev // TOGETHER, rows // TOGETHER, other_rows, 0)

    near = lax.broadcasted_iota(jnp.int32, (LANES, LANES), 1) < TILE
    chunks = rows // LANES

    def lay(n, carry):
        v = lax.div(n, chunks)
        chunk = lax.rem(n, chunks)
        base = (v * rows + chunk * LANES) * HALF
        for j in range(packed_tiles + 1):
            if j < packed_tiles:
                a = folded[pl.ds(base + 2 * j, LANES, stride=HALF), :]
                b = folded[pl.ds(base + 2 * j + 1, LANES, stride=HALF), :]
            else:
                a = b = corner[pl.ds(pl.multiple_of(v * rows + chunk * LANES, LANES), LANES), :]
            u0 = jnp.where(near, a, pltpu.roll(b, TILE, 1))
            u1 = jnp.where(near, pltpu.roll(a, TILE, 1), b)
            parts = split(u0) + split(u1)
            for k, value in enumerate(parts):
                at = pl.multiple_of(k * rows + chunk * LANES, LANES)
                left[v, pl.ds(at, LANES), j * LANES:(j + 1) * LANES] = value
        return carry

    lax.fori_loop(0, pairs * chunks, lay, 0)

    column = lax.broadcasted_iota(jnp.int32, (LANES, across), 0)
    for r in range(n_row):
        for v in range(pairs):

            def mark(n, carry):
                start = pl.multiple_of(n * LANES, LANES)
                value = jnp.where(column + n * LANES == perm_ref[r, v], 1.0, 0.0)
                hot[r, v, pl.ds(start, LANES), :] = value.astype(jnp.bfloat16)
                return carry

            lax.fori_loop(0, columns // LANES, mark, 0)

    even = lax.rem(lax.broadcasted_iota(jnp.int32, (rows, across), 1), GROUP) < GROUP // 2

    def place(v, r, fresh):
        high, low = split(theirs[v, r])
        value = jnp.concatenate([high, low], axis=0)
        value = lax.dot_general(value, hot[r, v], NT, preferred_element_type=jnp.float32)
        value = value[:s_dev] + value[s_dev:]
        total[...] = value if fresh else total[...] + value

    def place_mates(v):
        for there in mates:
            y_copy(v, there, there).wait_recv()
            place(v, there, False)

    for v in range(pairs):

        def landed(n, carry):
            there = target(n)
            c_copy(v, there, there).wait_recv()
            return carry

        lax.fori_loop(0, n_col - 1, landed, 0)
        both = lax.dot_general(left[v], recv[v], NT, preferred_element_type=jnp.float32)
        u0 = both[:rows] + both[rows:2 * rows]
        u1 = both[2 * rows:3 * rows] + both[3 * rows:]
        value = jnp.where(even, u0, u1)
        for block in range(rows // RB):
            q, r = divmod(block, n_row)
            mine[v, r, q * RB:(q + 1) * RB, :] = value[block * RB:(block + 1) * RB]
        for there in mates:
            y_copy(v, there, own).start()
        theirs[v, own] = mine[v, own]
        place(v, own, v == 0)
        if v > 0:
            place_mates(v - 1)
    place_mates(pairs - 1)

    out_cols = columns // n_col
    for c in range(n_col):
        placed[c] = total[:, c * out_cols:(c + 1) * out_cols]

    def give(n, carry):
        p_copy(target(n), me).start()
        return carry

    lax.fori_loop(0, n_col - 1, give, 0)
    summed = placed[me]
    for k in range(1, n_col):
        there = lax.rem(me + k, n_col)
        p_copy(there, there).wait_recv()
        summed = summed + arrived[there]
    out_ref[...] = summed

    def done(n, carry):
        there = target(n)
        for v in range(pairs):
            c_copy(v, there, me).wait_send()
        p_copy(there, me).wait_send()
        return carry

    lax.fori_loop(0, n_col - 1, done, 0)
    for there in mates:
        tile_copy(there, own).wait_send()
        slab_copy(there, own).wait_send()
        for v in range(pairs):
            y_copy(v, there, own).wait_send()


def body(n_row, n_col, primal, dual_inv, col_values, col_perm, slab_values, slab_tile):
    tile_count = col_values.shape[1]
    order = primal.shape[1]
    columns = col_perm.shape[1]
    s_dev = slab_values.shape[1]
    rows = n_row * s_dev
    keep = col_values.shape[2]
    block = lax.axis_index("col")
    part = tile_count // n_row
    width = part * TILE
    pairs = part // 2
    perm = lax.dynamic_index_in_dim(col_perm, block, 0, keepdims=False)
    perm = perm.reshape(n_row, pairs, 2, n_col, keep)
    perm = jnp.transpose(perm, (0, 1, 3, 2, 4)).reshape(n_row, pairs, 1, n_col * 2 * keep)
    col = col_values.reshape(n_col, tile_count // 2, GROUP, TILE * TILE)

    packed = TILE * TILE // 2 + LANES
    out_cols = columns // n_col
    across = n_col * GROUP
    vmem = pl.BlockSpec(memory_space=pltpu.VMEM)
    whole = pl.BlockSpec(memory_space=pl.ANY)
    dma = pltpu.SemaphoreType.DMA
    f32, bf16, i32 = jnp.float32, jnp.bfloat16, jnp.int32
    return pl.pallas_call(
        functools.partial(kernel, n_row, n_col),
        out_shape=jax.ShapeDtypeStruct((s_dev, out_cols), f32),
        in_specs=[pl.BlockSpec(memory_space=pltpu.SMEM), vmem, vmem, whole, whole, whole, whole],
        out_specs=vmem,
        scratch_shapes=[
            pltpu.VMEM((width, order), f32),
            pltpu.VMEM((order, width), f32),
            pltpu.VMEM((order // TILE, width, 2 * LANES), bf16),
            pltpu.VMEM((order // TILE, 2 * TILE, width), bf16),
            pltpu.VMEM((8, LANES), i32),
            pltpu.VMEM((n_row, 8, LANES), i32),
            pltpu.SMEM((n_row, 8, LANES), i32),
            pltpu.VMEM((n_row, s_dev, TILE * TILE), bf16),
            pltpu.VMEM((rows * TILE, LANES), f32),
            pltpu.VMEM((AHEAD, GROUP, TILE * TILE), bf16),
            pltpu.VMEM((n_col, pairs, GROUP, packed), bf16),
            pltpu.VMEM((pairs, across, packed), bf16),
            pltpu.VMEM((pairs * rows * HALF, LANES), f32),
            pltpu.VMEM((pairs * rows, LANES), f32),
            pltpu.VMEM((pairs, 4 * rows, packed), bf16),
            pltpu.VMEM((pairs, n_row, s_dev, across), f32),
            pltpu.VMEM((pairs, n_row, s_dev, across), f32),
            pltpu.VMEM((n_row, pairs, columns, across), bf16),
            pltpu.VMEM((s_dev, columns), f32),
            pltpu.VMEM((n_col, s_dev, out_cols), f32),
            pltpu.VMEM((n_col, s_dev, out_cols), f32),
            dma((AHEAD,)), dma((4,)), dma((pairs, n_col)), dma((pairs, n_col)),
            dma((n_row,)), dma((n_row,)), dma((n_row,)), dma((n_row,)),
            dma((pairs, n_row)), dma((pairs, n_row)), dma((n_col,)), dma((n_col,)),
        ],
        compiler_params=pltpu.CompilerParams(
            collective_id=0, has_side_effects=True, vmem_limit_bytes=60 * 1024 * 1024
        ),
    )(slab_tile, slab_tile, perm, primal, dual_inv, slab_values, col)


def solution(mesh):
    def run(*args):
        return body(mesh.shape["row"], mesh.shape["col"], *args)

    return jax.shard_map(
        run,
        mesh=mesh,
        in_specs=(
            P("col", None, None),
            P("col", None, None),
            P(None, None, "col", None),
            P(),
            P("col", "row", None),
            P("col", "row"),
        ),
        out_specs=P("row", "col"),
        check_vma=False,
    )
```

```python
import functools

import jax
import jax.numpy as jnp
from jax import lax
from jax.experimental import pallas as pl
from jax.experimental.pallas import tpu as pltpu
from jax.sharding import PartitionSpec as P

TILE = 64
HALF = TILE // 2
RB = 32
LANES = 128
GROUP = 16
ROLL = LANES - HALF
TOGETHER = 4
AHEAD = 16
MESH = pl.DeviceIdType.MESH
NT = (((1,), (1,)), ((), ()))


def split(value):
    high = value.astype(jnp.bfloat16)
    low = (value - high.astype(jnp.float32)).astype(jnp.bfloat16)
    return high, low


def kernel(
    n_row, n_col, own_tile, tile_ref, perm_ref, x_hbm, z_hbm, s_hbm, col_ref, out_ref,
    x_raw, z_raw, x_ref, z_ref, tile_out, tile_in, tile_all, s_raw, slab,
    raw, send, recv, folded, corner, left, mine, theirs, hot, total, placed, arrived, over_out, over_in,
    load_sem, in_sem, c_send, c_recv, s_send, s_recv, t_send, t_recv, y_send, y_recv, p_send, p_recv, o_send, o_recv,
):
    me = lax.axis_index("col")
    own = lax.axis_index("row")
    s_dev = s_hbm.shape[1]
    rows = n_row * s_dev
    pairs = send.shape[1]
    width = pairs * LANES
    packed_tiles = TILE * TILE // 2 // LANES
    across = n_col * GROUP
    columns = hot.shape[2]

    x_copy = pltpu.make_async_copy(x_hbm.at[0, pl.ds(own * width, width)], x_raw, in_sem.at[0])
    z_copy = pltpu.make_async_copy(
        z_hbm.at[0, :, pl.ds(pl.multiple_of(own * width, LANES), width)], z_raw, in_sem.at[1]
    )
    s_copy = pltpu.make_async_copy(s_hbm.at[0], s_raw.at[own], in_sem.at[2])
    x_copy.start()
    z_copy.start()
    s_copy.start()

    def offset(n):
        return n_col // 2 + lax.div(n + 1, 2) * (1 - 2 * lax.rem(n, 2))

    def target(n):
        return lax.rem(me + offset(n), n_col)

    def load(n):
        slot = lax.rem(n, AHEAD)
        return pltpu.make_async_copy(
            col_ref.at[target(lax.rem(n, n_col)), own * pairs + lax.div(n, n_col)],
            raw.at[slot], load_sem.at[slot],
        )

    steps = pairs * n_col
    for n in range(min(AHEAD - 1, steps)):
        load(n).start()

    barrier = pltpu.get_barrier_semaphore()
    for k in range(1, n_col):
        pl.semaphore_signal(barrier, inc=1, device_id={"col": lax.rem(me + k, n_col)}, device_id_type=MESH)
    for k in range(1, n_row):
        pl.semaphore_signal(barrier, inc=1, device_id={"row": lax.rem(own + k, n_row)}, device_id_type=MESH)

    tile_out[...] = jnp.zeros_like(tile_out)
    tile_out[0:1, 0:s_dev] = tile_ref[...]
    pl.semaphore_wait(barrier, n_col + n_row - 2)

    def row_copy(src, dst, out_sem, in_sem, there):
        return pltpu.make_async_remote_copy(
            src_ref=src, dst_ref=dst, send_sem=out_sem, recv_sem=in_sem,
            device_id={"row": there}, device_id_type=MESH,
        )

    def tile_copy(there, here):
        return row_copy(tile_out, tile_in.at[here], t_send.at[there], t_recv.at[here], there)

    def slab_copy(there, here):
        return row_copy(s_hbm.at[0], s_raw.at[here], s_send.at[there], s_recv.at[here], there)

    def y_copy(v, there, here):
        return row_copy(
            mine.at[v, there], theirs.at[v, here], y_send.at[v, there], y_recv.at[v, here], there
        )

    def c_copy(v, there, here):
        return pltpu.make_async_remote_copy(
            src_ref=send.at[there, v], dst_ref=recv.at[v, pl.ds(here * GROUP, GROUP)],
            send_sem=c_send.at[v, there], recv_sem=c_recv.at[v, here],
            device_id={"col": there}, device_id_type=MESH,
        )

    half_col = n_col // 2
    my_side = lax.div(me, half_col)
    my_place = lax.rem(me, half_col)
    far_side = 1 - my_side
    sides = (far_side, my_side)

    def p_copy(which, there, here):
        return pltpu.make_async_remote_copy(
            src_ref=placed.at[sides[which] * half_col + there], dst_ref=arrived.at[which, here],
            send_sem=p_send.at[which, there], recv_sem=p_recv.at[which, here],
            device_id={"col": my_side * half_col + there}, device_id_type=MESH,
        )

    over_copy = pltpu.make_async_remote_copy(
        src_ref=over_out, dst_ref=over_in, send_sem=o_send.at[0], recv_sem=o_recv.at[0],
        device_id={"col": far_side * half_col + my_place}, device_id_type=MESH,
    )

    mates = [lax.rem(own + k, n_row) for k in range(1, n_row)]
    for there in mates:
        tile_copy(there, own).start()
        slab_copy(there, own).start()

    lane = lax.broadcasted_iota(jnp.int32, (GROUP, LANES), 1)
    odd = jnp.where(lane >= TILE, 1, 0)
    entry = lane - odd * TILE

    def pack(slot, store):
        rest = jnp.zeros((GROUP, LANES), jnp.float32)
        for j in range(packed_tiles):
            upper = raw[slot, :, j * LANES:(j + 1) * LANES].astype(jnp.float32)
            start = (packed_tiles + j) * LANES
            lower = raw[slot, :, start:start + LANES].astype(jnp.float32)
            row = odd + 2 * j
            both = jnp.where(entry >= row, upper, pltpu.roll(lower, ROLL, 1))
            store(j, both.astype(jnp.bfloat16))
            rest = jnp.where(entry == row + HALF, lower, rest)
        store(packed_tiles, rest.astype(jnp.bfloat16))

    def outgoing(n, carry):
        @pl.when(n + AHEAD - 1 < steps)
        def _():
            load(n + AHEAD - 1).start()

        load(n).wait()
        v = lax.div(n, n_col)
        step = lax.rem(n, n_col)
        there = target(step)

        def store(j, value):
            send[there, v, :, j * LANES:(j + 1) * LANES] = value

        pack(lax.rem(n, AHEAD), store)

        @pl.when(step < n_col - 1)
        def _():
            c_copy(v, there, me).start()

        return carry

    lax.fori_loop(0, steps, outgoing, 0)
    for v in range(pairs):
        recv[v, pl.ds(pl.multiple_of(me * GROUP, GROUP), GROUP), :] = send[me, v]

    half = lax.broadcasted_iota(jnp.int32, (width, LANES), 1) < TILE
    x_copy.wait()
    for j in range(x_raw.shape[1] // LANES):
        a = x_raw[:, j * LANES:(j + 1) * LANES]
        b = pltpu.roll(a, TILE, 1)
        for k, value in enumerate((jnp.where(half, a, b), jnp.where(half, b, a))):
            high, low = split(value)
            x_ref[2 * j + k, :, :LANES] = high
            x_ref[2 * j + k, :, LANES:] = low
    z_copy.wait()

    def parts_of(t, carry):
        high, low = split(z_raw[pl.ds(pl.multiple_of(t * TILE, TILE), TILE), :])
        z_ref[t, :TILE] = high
        z_ref[t, TILE:] = low
        return carry

    lax.fori_loop(0, z_ref.shape[0], parts_of, 0)

    slab_half = lax.broadcasted_iota(jnp.int32, (s_dev, LANES), 1) < TILE

    def expand(r):
        for j in range(TILE * TILE // LANES):
            a = s_raw[r, :, j * LANES:(j + 1) * LANES].astype(jnp.float32)
            b = pltpu.roll(a, TILE, 1)
            slab[pl.ds(r * s_dev * TILE + 2 * j, s_dev, stride=TILE), :] = jnp.where(slab_half, a, b)
            slab[pl.ds(r * s_dev * TILE + 2 * j + 1, s_dev, stride=TILE), :] = jnp.where(slab_half, b, a)

    s_copy.wait()
    expand(own)

    wide = lax.broadcasted_iota(jnp.int32, (TILE, LANES), 1)
    first = wide < TILE
    e = lax.broadcasted_iota(jnp.int32, (HALF, LANES), 0)
    f = lax.broadcasted_iota(jnp.int32, (HALF, LANES), 1)
    f = jnp.where(f >= TILE, f - TILE, f)

    def terms(i, t):
        square = slab[pl.ds(pl.multiple_of(i * TILE, TILE), TILE), :].astype(jnp.bfloat16)
        panel = jnp.dot(square, z_ref[t], preferred_element_type=jnp.float32)
        high, low = split(panel)
        right = jnp.concatenate([high, low, high, low], axis=0)
        done = []
        for v in range(pairs):
            cut = slice(v * LANES, (v + 1) * LANES)
            term = jnp.dot(x_ref[t, cut], right[:, cut], preferred_element_type=jnp.float32)
            term = jnp.where(first, term[:TILE], term[TILE:])
            done.append(term.astype(jnp.bfloat16).astype(jnp.float32))
        if pairs % 2:
            done.append(done[-1])
        for v in range(0, len(done), 2):
            turned = jnp.concatenate(done[v:v + 2], axis=0).T
            crossed = pltpu.roll(turned, TILE, 1)
            done[v] += jnp.where(first, turned[:TILE], crossed[TILE:])
            done[v + 1] += jnp.where(first, crossed[:TILE], turned[TILE:])
        for v in range(pairs):
            upper, lower = done[v][:HALF], done[v][HALF:]
            both = jnp.where(f > e, upper, jnp.where(f < e, pltpu.roll(lower, ROLL, 1), 0.5 * upper))
            folded[pl.ds(pl.multiple_of((v * rows + i) * HALF, HALF), HALF), :] = both
            rest = jnp.sum(jnp.where(f == e + HALF, 0.5 * lower, 0.0), axis=0, keepdims=True)
            corner[pl.ds(v * rows + i, 1), :] = rest

    def first_rows(n, carry):
        for k in range(TOGETHER):
            inner = n * TOGETHER + k
            terms(own * s_dev + inner, own_tile[0, inner])
        return carry

    lax.fori_loop(0, s_dev // TOGETHER, first_rows, 0)
    for there in mates:
        tile_copy(there, there).wait_recv()
        slab_copy(there, there).wait_recv()
        expand(there)
    tile_in[own] = tile_out[...]
    tile_move = pltpu.make_async_copy(tile_in, tile_all, in_sem.at[3])
    tile_move.start()
    tile_move.wait()

    def other_rows(n, carry):
        for k in range(TOGETHER):
            at = n * TOGETHER + k
            there = lax.rem(own + lax.div(at, s_dev), n_row)
            inner = lax.rem(at, s_dev)
            terms(there * s_dev + inner, tile_all[there, 0, inner])
        return carry

    lax.fori_loop(s_dev // TOGETHER, rows // TOGETHER, other_rows, 0)

    near = lax.broadcasted_iota(jnp.int32, (LANES, LANES), 1) < TILE
    chunks = rows // LANES

    def lay(n, carry):
        v = lax.div(n, chunks)
        chunk = lax.rem(n, chunks)
        base = (v * rows + chunk * LANES) * HALF
        for j in range(packed_tiles + 1):
            if j < packed_tiles:
                a = folded[pl.ds(base + 2 * j, LANES, stride=HALF), :]
                b = folded[pl.ds(base + 2 * j + 1, LANES, stride=HALF), :]
            else:
                a = b = corner[pl.ds(pl.multiple_of(v * rows + chunk * LANES, LANES), LANES), :]
            u0 = jnp.where(near, a, pltpu.roll(b, TILE, 1))
            u1 = jnp.where(near, pltpu.roll(a, TILE, 1), b)
            parts = split(u0) + split(u1)
            for k, value in enumerate(parts):
                at = pl.multiple_of(k * rows + chunk * LANES, LANES)
                left[v, pl.ds(at, LANES), j * LANES:(j + 1) * LANES] = value
        return carry

    lax.fori_loop(0, pairs * chunks, lay, 0)

    column = lax.broadcasted_iota(jnp.int32, (LANES, across), 0)
    for r in range(n_row):
        for v in range(pairs):

            def mark(n, carry):
                start = pl.multiple_of(n * LANES, LANES)
                value = jnp.where(column + n * LANES == perm_ref[r, v], 1.0, 0.0)
                hot[r, v, pl.ds(start, LANES), :] = value.astype(jnp.bfloat16)
                return carry

            lax.fori_loop(0, columns // LANES, mark, 0)

    even = lax.rem(lax.broadcasted_iota(jnp.int32, (rows, across), 1), GROUP) < GROUP // 2

    def place(v, r, fresh):
        high, low = split(theirs[v, r])
        value = jnp.concatenate([high, low], axis=0)
        value = lax.dot_general(value, hot[r, v], NT, preferred_element_type=jnp.float32)
        value = value[:s_dev] + value[s_dev:]
        total[...] = value if fresh else total[...] + value

    def place_mates(v):
        for there in mates:
            y_copy(v, there, there).wait_recv()
            place(v, there, False)

    for v in range(pairs):

        def landed(n, carry):
            there = target(n)
            c_copy(v, there, there).wait_recv()
            return carry

        lax.fori_loop(0, n_col - 1, landed, 0)
        both = lax.dot_general(left[v], recv[v], NT, preferred_element_type=jnp.float32)
        u0 = both[:rows] + both[rows:2 * rows]
        u1 = both[2 * rows:3 * rows] + both[3 * rows:]
        value = jnp.where(even, u0, u1)
        for block in range(rows // RB):
            q, r = divmod(block, n_row)
            mine[v, r, q * RB:(q + 1) * RB, :] = value[block * RB:(block + 1) * RB]
        for there in mates:
            y_copy(v, there, own).start()
        theirs[v, own] = mine[v, own]
        place(v, own, v == 0)
        if v > 0:
            place_mates(v - 1)
    place_mates(pairs - 1)

    out_cols = columns // n_col
    for c in range(n_col):
        placed[c] = total[:, c * out_cols:(c + 1) * out_cols]

    near_ones = [lax.rem(my_place + k, half_col) for k in range(1, half_col)]
    for which in range(2):
        for there in near_ones:
            p_copy(which, there, my_place).start()
    summed = placed[far_side * half_col + my_place]
    for there in near_ones:
        p_copy(0, there, there).wait_recv()
        summed = summed + arrived[0, there]
    over_out[...] = summed
    over_copy.start()
    summed = placed[me]
    for there in near_ones:
        p_copy(1, there, there).wait_recv()
        summed = summed + arrived[1, there]
    over_copy.wait_recv()
    out_ref[...] = summed + over_in[...]
    over_copy.wait_send()
    for which in range(2):
        for there in near_ones:
            p_copy(which, there, my_place).wait_send()

    def done(n, carry):
        there = target(n)
        for v in range(pairs):
            c_copy(v, there, me).wait_send()
        return carry

    lax.fori_loop(0, n_col - 1, done, 0)
    for there in mates:
        tile_copy(there, own).wait_send()
        slab_copy(there, own).wait_send()
        for v in range(pairs):
            y_copy(v, there, own).wait_send()


def body(n_row, n_col, primal, dual_inv, col_values, col_perm, slab_values, slab_tile):
    tile_count = col_values.shape[1]
    order = primal.shape[1]
    columns = col_perm.shape[1]
    s_dev = slab_values.shape[1]
    rows = n_row * s_dev
    keep = col_values.shape[2]
    block = lax.axis_index("col")
    part = tile_count // n_row
    width = part * TILE
    pairs = part // 2
    perm = lax.dynamic_index_in_dim(col_perm, block, 0, keepdims=False)
    perm = perm.reshape(n_row, pairs, 2, n_col, keep)
    perm = jnp.transpose(perm, (0, 1, 3, 2, 4)).reshape(n_row, pairs, 1, n_col * 2 * keep)
    col = col_values.reshape(n_col, tile_count // 2, GROUP, TILE * TILE)

    packed = TILE * TILE // 2 + LANES
    out_cols = columns // n_col
    across = n_col * GROUP
    vmem = pl.BlockSpec(memory_space=pltpu.VMEM)
    whole = pl.BlockSpec(memory_space=pl.ANY)
    dma = pltpu.SemaphoreType.DMA
    f32, bf16, i32 = jnp.float32, jnp.bfloat16, jnp.int32
    return pl.pallas_call(
        functools.partial(kernel, n_row, n_col),
        out_shape=jax.ShapeDtypeStruct((s_dev, out_cols), f32),
        in_specs=[pl.BlockSpec(memory_space=pltpu.SMEM), vmem, vmem, whole, whole, whole, whole],
        out_specs=vmem,
        scratch_shapes=[
            pltpu.VMEM((width, order), f32),
            pltpu.VMEM((order, width), f32),
            pltpu.VMEM((order // TILE, width, 2 * LANES), bf16),
            pltpu.VMEM((order // TILE, 2 * TILE, width), bf16),
            pltpu.VMEM((8, LANES), i32),
            pltpu.VMEM((n_row, 8, LANES), i32),
            pltpu.SMEM((n_row, 8, LANES), i32),
            pltpu.VMEM((n_row, s_dev, TILE * TILE), bf16),
            pltpu.VMEM((rows * TILE, LANES), f32),
            pltpu.VMEM((AHEAD, GROUP, TILE * TILE), bf16),
            pltpu.VMEM((n_col, pairs, GROUP, packed), bf16),
            pltpu.VMEM((pairs, across, packed), bf16),
            pltpu.VMEM((pairs * rows * HALF, LANES), f32),
            pltpu.VMEM((pairs * rows, LANES), f32),
            pltpu.VMEM((pairs, 4 * rows, packed), bf16),
            pltpu.VMEM((pairs, n_row, s_dev, across), f32),
            pltpu.VMEM((pairs, n_row, s_dev, across), f32),
            pltpu.VMEM((n_row, pairs, columns, across), bf16),
            pltpu.VMEM((s_dev, columns), f32),
            pltpu.VMEM((n_col, s_dev, out_cols), f32),
            pltpu.VMEM((2, n_col // 2, s_dev, out_cols), f32),
            pltpu.VMEM((s_dev, out_cols), f32),
            pltpu.VMEM((s_dev, out_cols), f32),
            dma((AHEAD,)), dma((4,)), dma((pairs, n_col)), dma((pairs, n_col)),
            dma((n_row,)), dma((n_row,)), dma((n_row,)), dma((n_row,)),
            dma((pairs, n_row)), dma((pairs, n_row)), dma((2, n_col // 2)), dma((2, n_col // 2)),
            dma((1,)), dma((1,)),
        ],
        compiler_params=pltpu.CompilerParams(
            collective_id=0, has_side_effects=True, vmem_limit_bytes=60 * 1024 * 1024
        ),
    )(slab_tile, slab_tile, perm, primal, dual_inv, slab_values, col)


def solution(mesh):
    def run(*args):
        return body(mesh.shape["row"], mesh.shape["col"], *args)

    return jax.shard_map(
        run,
        mesh=mesh,
        in_specs=(
            P("col", None, None),
            P("col", None, None),
            P(None, None, "col", None),
            P(),
            P("col", "row", None),
            P("col", "row"),
        ),
        out_specs=P("row", "col"),
        check_vma=False,
    )
```

```python
import functools

import jax
import jax.numpy as jnp
from jax import lax
from jax.experimental import pallas as pl
from jax.experimental.pallas import tpu as pltpu
from jax.sharding import PartitionSpec as P

TILE = 64
HALF = TILE // 2
RB = 32
LANES = 128
GROUP = 16
ROLL = LANES - HALF
TOGETHER = 4
AHEAD = 16
MESH = pl.DeviceIdType.MESH
NT = (((1,), (1,)), ((), ()))


def split(value):
    high = value.astype(jnp.bfloat16)
    low = (value - high.astype(jnp.float32)).astype(jnp.bfloat16)
    return high, low


def kernel(
    n_row, n_col, own_tile, tile_ref, perm_ref, x_hbm, z_hbm, s_hbm, col_ref, out_ref,
    x_raw, z_raw, x_ref, z_ref, tile_out, tile_in, tile_all, s_raw, slab,
    raw, send, recv, folded, corner, left, mine, theirs, hot, total, placed, arrived, over_out, over_in,
    rest_sum, rest_out, rest_in,
    load_sem, in_sem, c_send, c_recv, s_send, s_recv, t_send, t_recv, y_send, y_recv, p_send, p_recv, o_send, o_recv, r_send, r_recv,
):
    me = lax.axis_index("col")
    own = lax.axis_index("row")
    s_dev = s_hbm.shape[1]
    rows = n_row * s_dev
    pairs = send.shape[1]
    width = pairs * LANES
    packed_tiles = TILE * TILE // 2 // LANES
    across = n_col * GROUP
    columns = hot.shape[2]

    x_copy = pltpu.make_async_copy(x_hbm.at[0, pl.ds(own * width, width)], x_raw, in_sem.at[0])
    z_copy = pltpu.make_async_copy(
        z_hbm.at[0, :, pl.ds(pl.multiple_of(own * width, LANES), width)], z_raw, in_sem.at[1]
    )
    s_copy = pltpu.make_async_copy(s_hbm.at[0], s_raw.at[own], in_sem.at[2])
    x_copy.start()
    z_copy.start()
    s_copy.start()

    def offset(n):
        return n_col // 2 + lax.div(n + 1, 2) * (1 - 2 * lax.rem(n, 2))

    def target(n):
        return lax.rem(me + offset(n), n_col)

    def load(n):
        slot = lax.rem(n, AHEAD)
        return pltpu.make_async_copy(
            col_ref.at[target(lax.rem(n, n_col)), own * pairs + lax.div(n, n_col)],
            raw.at[slot], load_sem.at[slot],
        )

    steps = pairs * n_col
    for n in range(min(AHEAD - 1, steps)):
        load(n).start()

    barrier = pltpu.get_barrier_semaphore()
    for k in range(1, n_col):
        pl.semaphore_signal(barrier, inc=1, device_id={"col": lax.rem(me + k, n_col)}, device_id_type=MESH)
    for k in range(1, n_row):
        pl.semaphore_signal(barrier, inc=1, device_id={"row": lax.rem(own + k, n_row)}, device_id_type=MESH)

    tile_out[...] = jnp.zeros_like(tile_out)
    tile_out[0:1, 0:s_dev] = tile_ref[...]
    pl.semaphore_wait(barrier, n_col + n_row - 2)

    def row_copy(src, dst, out_sem, in_sem, there):
        return pltpu.make_async_remote_copy(
            src_ref=src, dst_ref=dst, send_sem=out_sem, recv_sem=in_sem,
            device_id={"row": there}, device_id_type=MESH,
        )

    def tile_copy(there, here):
        return row_copy(tile_out, tile_in.at[here], t_send.at[there], t_recv.at[here], there)

    def slab_copy(there, here):
        return row_copy(s_hbm.at[0], s_raw.at[here], s_send.at[there], s_recv.at[here], there)

    def y_copy(v, there, here):
        return row_copy(
            mine.at[v, there], theirs.at[v, here], y_send.at[v, there], y_recv.at[v, here], there
        )

    def c_copy(v, there, here):
        return pltpu.make_async_remote_copy(
            src_ref=send.at[there, v], dst_ref=recv.at[v, pl.ds(here * GROUP, GROUP)],
            send_sem=c_send.at[v, there], recv_sem=c_recv.at[v, here],
            device_id={"col": there}, device_id_type=MESH,
        )

    half_col = n_col // 2
    my_side = lax.div(me, half_col)
    my_place = lax.rem(me, half_col)
    far_side = 1 - my_side
    sides = (far_side, my_side)

    def p_copy(which, there, here):
        return pltpu.make_async_remote_copy(
            src_ref=placed.at[sides[which] * half_col + there], dst_ref=arrived.at[which, here],
            send_sem=p_send.at[which, there], recv_sem=p_recv.at[which, here],
            device_id={"col": my_side * half_col + there}, device_id_type=MESH,
        )

    over_copy = pltpu.make_async_remote_copy(
        src_ref=over_out, dst_ref=over_in, send_sem=o_send.at[0], recv_sem=o_recv.at[0],
        device_id={"col": far_side * half_col + my_place}, device_id_type=MESH,
    )

    mates = [lax.rem(own + k, n_row) for k in range(1, n_row)]
    for there in mates:
        tile_copy(there, own).start()
        slab_copy(there, own).start()

    lane = lax.broadcasted_iota(jnp.int32, (GROUP, LANES), 1)
    odd = jnp.where(lane >= TILE, 1, 0)
    entry = lane - odd * TILE

    def pack(slot, store):
        rest = jnp.zeros((GROUP, LANES), jnp.float32)
        for j in range(packed_tiles):
            upper = raw[slot, :, j * LANES:(j + 1) * LANES].astype(jnp.float32)
            start = (packed_tiles + j) * LANES
            lower = raw[slot, :, start:start + LANES].astype(jnp.float32)
            row = odd + 2 * j
            both = jnp.where(entry >= row, upper, pltpu.roll(lower, ROLL, 1))
            store(j, both.astype(jnp.bfloat16))
            rest = jnp.where(entry == row + HALF, lower, rest)
        return rest

    def r_copy(there, here):
        return pltpu.make_async_remote_copy(
            src_ref=rest_out.at[there], dst_ref=rest_in.at[pl.ds(here * GROUP, GROUP)],
            send_sem=r_send.at[there], recv_sem=r_recv.at[here],
            device_id={"col": there}, device_id_type=MESH,
        )

    for v in range(pairs):

        def outgoing(step, carry):
            n = v * n_col + step

            @pl.when(n + AHEAD - 1 < steps)
            def _():
                load(n + AHEAD - 1).start()

            load(n).wait()
            there = target(step)

            def store(j, value):
                send[there, v, :, j * LANES:(j + 1) * LANES] = value

            rest = pack(lax.rem(n, AHEAD), store)
            if v == 0:
                rest_sum[there] = rest

                @pl.when(step < n_col - 1)
                def _():
                    c_copy(v, there, me).start()
            else:
                rest_sum[there] += pltpu.roll(rest, v * HALF, 1)
            return carry

        lax.fori_loop(0, n_col, outgoing, 0)

    rest_out[...] = rest_sum[...].astype(jnp.bfloat16)

    def rests(step, carry):
        r_copy(target(step), me).start()
        return carry

    lax.fori_loop(0, n_col - 1, rests, 0)
    for v in range(1, pairs):

        def later(step, carry):
            c_copy(v, target(step), me).start()
            return carry

        lax.fori_loop(0, n_col - 1, later, 0)
    my_rows = pl.ds(pl.multiple_of(me * GROUP, GROUP), GROUP)
    for v in range(pairs):
        recv[v, my_rows, :] = send[me, v]
    rest_in[my_rows, :] = rest_out[me]

    half = lax.broadcasted_iota(jnp.int32, (width, LANES), 1) < TILE
    x_copy.wait()
    for j in range(x_raw.shape[1] // LANES):
        a = x_raw[:, j * LANES:(j + 1) * LANES]
        b = pltpu.roll(a, TILE, 1)
        for k, value in enumerate((jnp.where(half, a, b), jnp.where(half, b, a))):
            high, low = split(value)
            x_ref[2 * j + k, :, :LANES] = high
            x_ref[2 * j + k, :, LANES:] = low
    z_copy.wait()

    def parts_of(t, carry):
        high, low = split(z_raw[pl.ds(pl.multiple_of(t * TILE, TILE), TILE), :])
        z_ref[t, :TILE] = high
        z_ref[t, TILE:] = low
        return carry

    lax.fori_loop(0, z_ref.shape[0], parts_of, 0)

    slab_half = lax.broadcasted_iota(jnp.int32, (s_dev, LANES), 1) < TILE

    def expand(r):
        for j in range(TILE * TILE // LANES):
            a = s_raw[r, :, j * LANES:(j + 1) * LANES].astype(jnp.float32)
            b = pltpu.roll(a, TILE, 1)
            slab[pl.ds(r * s_dev * TILE + 2 * j, s_dev, stride=TILE), :] = jnp.where(slab_half, a, b)
            slab[pl.ds(r * s_dev * TILE + 2 * j + 1, s_dev, stride=TILE), :] = jnp.where(slab_half, b, a)

    s_copy.wait()
    expand(own)

    wide = lax.broadcasted_iota(jnp.int32, (TILE, LANES), 1)
    first = wide < TILE
    e = lax.broadcasted_iota(jnp.int32, (HALF, LANES), 0)
    f = lax.broadcasted_iota(jnp.int32, (HALF, LANES), 1)
    f = jnp.where(f >= TILE, f - TILE, f)

    def terms(i, t):
        square = slab[pl.ds(pl.multiple_of(i * TILE, TILE), TILE), :].astype(jnp.bfloat16)
        panel = jnp.dot(square, z_ref[t], preferred_element_type=jnp.float32)
        high, low = split(panel)
        right = jnp.concatenate([high, low, high, low], axis=0)
        done = []
        for v in range(pairs):
            cut = slice(v * LANES, (v + 1) * LANES)
            term = jnp.dot(x_ref[t, cut], right[:, cut], preferred_element_type=jnp.float32)
            term = jnp.where(first, term[:TILE], term[TILE:])
            done.append(term.astype(jnp.bfloat16).astype(jnp.float32))
        if pairs % 2:
            done.append(done[-1])
        for v in range(0, len(done), 2):
            turned = jnp.concatenate(done[v:v + 2], axis=0).T
            crossed = pltpu.roll(turned, TILE, 1)
            done[v] += jnp.where(first, turned[:TILE], crossed[TILE:])
            done[v + 1] += jnp.where(first, crossed[:TILE], turned[TILE:])
        for v in range(pairs):
            upper, lower = done[v][:HALF], done[v][HALF:]
            both = jnp.where(f > e, upper, jnp.where(f < e, pltpu.roll(lower, ROLL, 1), 0.5 * upper))
            folded[pl.ds(pl.multiple_of((v * rows + i) * HALF, HALF), HALF), :] = both
            rest = jnp.sum(jnp.where(f == e + HALF, 0.5 * lower, 0.0), axis=0, keepdims=True)
            corner[pl.ds(v * rows + i, 1), :] = rest

    def first_rows(n, carry):
        for k in range(TOGETHER):
            inner = n * TOGETHER + k
            terms(own * s_dev + inner, own_tile[0, inner])
        return carry

    lax.fori_loop(0, s_dev // TOGETHER, first_rows, 0)
    for there in mates:
        tile_copy(there, there).wait_recv()
        slab_copy(there, there).wait_recv()
        expand(there)
    tile_in[own] = tile_out[...]
    tile_move = pltpu.make_async_copy(tile_in, tile_all, in_sem.at[3])
    tile_move.start()
    tile_move.wait()

    def other_rows(n, carry):
        for k in range(TOGETHER):
            at = n * TOGETHER + k
            there = lax.rem(own + lax.div(at, s_dev), n_row)
            inner = lax.rem(at, s_dev)
            terms(there * s_dev + inner, tile_all[there, 0, inner])
        return carry

    lax.fori_loop(s_dev // TOGETHER, rows // TOGETHER, other_rows, 0)

    spot = lax.broadcasted_iota(jnp.int32, (LANES, LANES), 1)
    near = spot < TILE
    parity = jnp.where(near, 0, 1) == lax.rem(spot, 2)
    for v in range(pairs):

        def lay(chunk, carry):
            base = (v * rows + chunk * LANES) * HALF
            for j in range(packed_tiles + 1):
                if j < packed_tiles:
                    a = folded[pl.ds(base + 2 * j, LANES, stride=HALF), :]
                    b = folded[pl.ds(base + 2 * j + 1, LANES, stride=HALF), :]
                else:
                    a = b = corner[pl.ds(pl.multiple_of(v * rows + chunk * LANES, LANES), LANES), :]
                u0 = jnp.where(near, a, pltpu.roll(b, TILE, 1))
                u1 = jnp.where(near, pltpu.roll(a, TILE, 1), b)
                if j == packed_tiles:
                    u0 = jnp.where(parity, u0, 0.0)
                    u1 = jnp.where(parity, u1, 0.0)
                    if v:
                        u0 = pltpu.roll(u0, v * HALF, 1)
                        u1 = pltpu.roll(u1, v * HALF, 1)
                parts = split(u0) + split(u1)
                for k, value in enumerate(parts):
                    at = pl.multiple_of(k * rows + chunk * LANES, LANES)
                    left[v, pl.ds(at, LANES), j * LANES:(j + 1) * LANES] = value
            return carry

        lax.fori_loop(0, rows // LANES, lay, 0)

    column = lax.broadcasted_iota(jnp.int32, (LANES, across), 0)
    for r in range(n_row):
        for v in range(pairs):

            def mark(n, carry):
                start = pl.multiple_of(n * LANES, LANES)
                value = jnp.where(column + n * LANES == perm_ref[r, v], 1.0, 0.0)
                hot[r, v, pl.ds(start, LANES), :] = value.astype(jnp.bfloat16)
                return carry

            lax.fori_loop(0, columns // LANES, mark, 0)

    even = lax.rem(lax.broadcasted_iota(jnp.int32, (rows, across), 1), GROUP) < GROUP // 2

    def place(v, r, fresh):
        high, low = split(theirs[v, r])
        value = jnp.concatenate([high, low], axis=0)
        value = lax.dot_general(value, hot[r, v], NT, preferred_element_type=jnp.float32)
        value = value[:s_dev] + value[s_dev:]
        total[...] = value if fresh else total[...] + value

    def place_mates(v):
        for there in mates:
            y_copy(v, there, there).wait_recv()
            place(v, there, False)

    for v in range(pairs):

        def landed(n, carry):
            there = target(n)
            c_copy(v, there, there).wait_recv()
            if v == 0:
                r_copy(there, there).wait_recv()
            return carry

        lax.fori_loop(0, n_col - 1, landed, 0)
        most = packed_tiles * LANES
        both = lax.dot_general(left[v, :, :most], recv[v], NT, preferred_element_type=jnp.float32)
        both += lax.dot_general(left[v, :, most:], rest_in[...], NT, preferred_element_type=jnp.float32)
        u0 = both[:rows] + both[rows:2 * rows]
        u1 = both[2 * rows:3 * rows] + both[3 * rows:]
        value = jnp.where(even, u0, u1)
        for block in range(rows // RB):
            q, r = divmod(block, n_row)
            mine[v, r, q * RB:(q + 1) * RB, :] = value[block * RB:(block + 1) * RB]
        for there in mates:
            y_copy(v, there, own).start()
        theirs[v, own] = mine[v, own]
        place(v, own, v == 0)
        if v > 0:
            place_mates(v - 1)
    place_mates(pairs - 1)

    out_cols = columns // n_col
    for c in range(n_col):
        placed[c] = total[:, c * out_cols:(c + 1) * out_cols]

    near_ones = [lax.rem(my_place + k, half_col) for k in range(1, half_col)]
    for which in range(2):
        for there in near_ones:
            p_copy(which, there, my_place).start()
    summed = placed[far_side * half_col + my_place]
    for there in near_ones:
        p_copy(0, there, there).wait_recv()
        summed = summed + arrived[0, there]
    over_out[...] = summed
    over_copy.start()
    summed = placed[me]
    for there in near_ones:
        p_copy(1, there, there).wait_recv()
        summed = summed + arrived[1, there]
    over_copy.wait_recv()
    out_ref[...] = summed + over_in[...]
    over_copy.wait_send()
    for which in range(2):
        for there in near_ones:
            p_copy(which, there, my_place).wait_send()

    def done(n, carry):
        there = target(n)
        for v in range(pairs):
            c_copy(v, there, me).wait_send()
        r_copy(there, me).wait_send()
        return carry

    lax.fori_loop(0, n_col - 1, done, 0)
    for there in mates:
        tile_copy(there, own).wait_send()
        slab_copy(there, own).wait_send()
        for v in range(pairs):
            y_copy(v, there, own).wait_send()


def body(n_row, n_col, primal, dual_inv, col_values, col_perm, slab_values, slab_tile):
    tile_count = col_values.shape[1]
    order = primal.shape[1]
    columns = col_perm.shape[1]
    s_dev = slab_values.shape[1]
    rows = n_row * s_dev
    keep = col_values.shape[2]
    block = lax.axis_index("col")
    part = tile_count // n_row
    width = part * TILE
    pairs = part // 2
    perm = lax.dynamic_index_in_dim(col_perm, block, 0, keepdims=False)
    perm = perm.reshape(n_row, pairs, 2, n_col, keep)
    perm = jnp.transpose(perm, (0, 1, 3, 2, 4)).reshape(n_row, pairs, 1, n_col * 2 * keep)
    col = col_values.reshape(n_col, tile_count // 2, GROUP, TILE * TILE)

    packed = TILE * TILE // 2 + LANES
    out_cols = columns // n_col
    across = n_col * GROUP
    vmem = pl.BlockSpec(memory_space=pltpu.VMEM)
    whole = pl.BlockSpec(memory_space=pl.ANY)
    dma = pltpu.SemaphoreType.DMA
    f32, bf16, i32 = jnp.float32, jnp.bfloat16, jnp.int32
    return pl.pallas_call(
        functools.partial(kernel, n_row, n_col),
        out_shape=jax.ShapeDtypeStruct((s_dev, out_cols), f32),
        in_specs=[pl.BlockSpec(memory_space=pltpu.SMEM), vmem, vmem, whole, whole, whole, whole],
        out_specs=vmem,
        scratch_shapes=[
            pltpu.VMEM((width, order), f32),
            pltpu.VMEM((order, width), f32),
            pltpu.VMEM((order // TILE, width, 2 * LANES), bf16),
            pltpu.VMEM((order // TILE, 2 * TILE, width), bf16),
            pltpu.VMEM((8, LANES), i32),
            pltpu.VMEM((n_row, 8, LANES), i32),
            pltpu.SMEM((n_row, 8, LANES), i32),
            pltpu.VMEM((n_row, s_dev, TILE * TILE), bf16),
            pltpu.VMEM((rows * TILE, LANES), f32),
            pltpu.VMEM((AHEAD, GROUP, TILE * TILE), bf16),
            pltpu.VMEM((n_col, pairs, GROUP, packed - LANES), bf16),
            pltpu.VMEM((pairs, across, packed - LANES), bf16),
            pltpu.VMEM((pairs * rows * HALF, LANES), f32),
            pltpu.VMEM((pairs * rows, LANES), f32),
            pltpu.VMEM((pairs, 4 * rows, packed), bf16),
            pltpu.VMEM((pairs, n_row, s_dev, across), f32),
            pltpu.VMEM((pairs, n_row, s_dev, across), f32),
            pltpu.VMEM((n_row, pairs, columns, across), bf16),
            pltpu.VMEM((s_dev, columns), f32),
            pltpu.VMEM((n_col, s_dev, out_cols), f32),
            pltpu.VMEM((2, n_col // 2, s_dev, out_cols), f32),
            pltpu.VMEM((s_dev, out_cols), f32),
            pltpu.VMEM((s_dev, out_cols), f32),
            pltpu.VMEM((n_col, GROUP, LANES), f32),
            pltpu.VMEM((n_col, GROUP, LANES), bf16),
            pltpu.VMEM((across, LANES), bf16),
            dma((AHEAD,)), dma((4,)), dma((pairs, n_col)), dma((pairs, n_col)),
            dma((n_row,)), dma((n_row,)), dma((n_row,)), dma((n_row,)),
            dma((pairs, n_row)), dma((pairs, n_row)), dma((2, n_col // 2)), dma((2, n_col // 2)),
            dma((1,)), dma((1,)), dma((n_col,)), dma((n_col,)),
        ],
        compiler_params=pltpu.CompilerParams(
            collective_id=0, has_side_effects=True, vmem_limit_bytes=60 * 1024 * 1024
        ),
    )(slab_tile, slab_tile, perm, primal, dual_inv, slab_values, col)


def solution(mesh):
    def run(*args):
        return body(mesh.shape["row"], mesh.shape["col"], *args)

    return jax.shard_map(
        run,
        mesh=mesh,
        in_specs=(
            P("col", None, None),
            P("col", None, None),
            P(None, None, "col", None),
            P(),
            P("col", "row", None),
            P("col", "row"),
        ),
        out_specs=P("row", "col"),
        check_vma=False,
    )
```

```python
import functools

import jax
import jax.numpy as jnp
from jax import lax
from jax.experimental import pallas as pl
from jax.experimental.pallas import tpu as pltpu
from jax.sharding import PartitionSpec as P

TILE = 64
HALF = TILE // 2
RB = 32
LANES = 128
GROUP = 16
ROLL = LANES - HALF
TOGETHER = 4
AHEAD = 16
MESH = pl.DeviceIdType.MESH
NT = (((1,), (1,)), ((), ()))


def split(value):
    high = value.astype(jnp.bfloat16)
    low = (value - high.astype(jnp.float32)).astype(jnp.bfloat16)
    return high, low


def kernel(
    n_row, n_col, own_tile, tile_ref, perm_hbm, x_hbm, z_hbm, s_hbm, col_ref, out_ref,
    x_raw, z_raw, x_ref, z_ref, tile_out, tile_in, tile_all, s_raw, slab,
    raw, send, recv, folded, corner, left, mine, theirs, hot, total, placed, arrived, over_out, over_in,
    rest_sum, rest_out, rest_in, perm_raw, perm_ref,
    load_sem, in_sem, c_send, c_recv, s_send, s_recv, t_send, t_recv, y_send, y_recv, p_send, p_recv, o_send, o_recv, r_send, r_recv,
):
    me = lax.axis_index("col")
    own = lax.axis_index("row")
    s_dev = s_hbm.shape[1]
    rows = n_row * s_dev
    pairs = send.shape[1]
    width = pairs * LANES
    packed_tiles = TILE * TILE // 2 // LANES
    across = n_col * GROUP
    columns = hot.shape[2]

    x_copy = pltpu.make_async_copy(x_hbm.at[0, pl.ds(own * width, width)], x_raw, in_sem.at[0])
    z_copy = pltpu.make_async_copy(
        z_hbm.at[0, :, pl.ds(pl.multiple_of(own * width, LANES), width)], z_raw, in_sem.at[1]
    )
    s_copy = pltpu.make_async_copy(s_hbm.at[0], s_raw.at[own], in_sem.at[2])
    x_copy.start()
    z_copy.start()
    s_copy.start()
    perm_copy = pltpu.make_async_copy(perm_hbm.at[pl.ds(me, 1)], perm_raw, in_sem.at[4])
    perm_copy.start()

    def offset(n):
        return n_col // 2 + lax.div(n + 1, 2) * (1 - 2 * lax.rem(n, 2))

    def target(n):
        return lax.rem(me + offset(n), n_col)

    def load(n):
        slot = lax.rem(n, AHEAD)
        return pltpu.make_async_copy(
            col_ref.at[target(lax.rem(n, n_col)), own * pairs + lax.div(n, n_col)],
            raw.at[slot], load_sem.at[slot],
        )

    steps = pairs * n_col
    for n in range(min(AHEAD - 1, steps)):
        load(n).start()

    barrier = pltpu.get_barrier_semaphore()
    for k in range(1, n_col):
        pl.semaphore_signal(barrier, inc=1, device_id={"col": lax.rem(me + k, n_col)}, device_id_type=MESH)
    for k in range(1, n_row):
        pl.semaphore_signal(barrier, inc=1, device_id={"row": lax.rem(own + k, n_row)}, device_id_type=MESH)

    tile_out[...] = jnp.zeros_like(tile_out)
    tile_out[0:1, 0:s_dev] = tile_ref[...]
    pl.semaphore_wait(barrier, n_col + n_row - 2)

    def row_copy(src, dst, out_sem, in_sem, there):
        return pltpu.make_async_remote_copy(
            src_ref=src, dst_ref=dst, send_sem=out_sem, recv_sem=in_sem,
            device_id={"row": there}, device_id_type=MESH,
        )

    def tile_copy(there, here):
        return row_copy(tile_out, tile_in.at[here], t_send.at[there], t_recv.at[here], there)

    def slab_copy(there, here):
        return row_copy(s_hbm.at[0], s_raw.at[here], s_send.at[there], s_recv.at[here], there)

    def y_copy(v, there, here):
        return row_copy(
            mine.at[v, there], theirs.at[v, here], y_send.at[v, there], y_recv.at[v, here], there
        )

    def c_copy(v, there, here):
        return pltpu.make_async_remote_copy(
            src_ref=send.at[there, v], dst_ref=recv.at[v, pl.ds(here * GROUP, GROUP)],
            send_sem=c_send.at[v, there], recv_sem=c_recv.at[v, here],
            device_id={"col": there}, device_id_type=MESH,
        )

    half_col = n_col // 2
    my_side = lax.div(me, half_col)
    my_place = lax.rem(me, half_col)
    far_side = 1 - my_side
    sides = (far_side, my_side)

    def p_copy(which, there, here):
        return pltpu.make_async_remote_copy(
            src_ref=placed.at[sides[which] * half_col + there], dst_ref=arrived.at[which, here],
            send_sem=p_send.at[which, there], recv_sem=p_recv.at[which, here],
            device_id={"col": my_side * half_col + there}, device_id_type=MESH,
        )

    over_copy = pltpu.make_async_remote_copy(
        src_ref=over_out, dst_ref=over_in, send_sem=o_send.at[0], recv_sem=o_recv.at[0],
        device_id={"col": far_side * half_col + my_place}, device_id_type=MESH,
    )

    mates = [lax.rem(own + k, n_row) for k in range(1, n_row)]
    for there in mates:
        tile_copy(there, own).start()
        slab_copy(there, own).start()

    lane = lax.broadcasted_iota(jnp.int32, (GROUP, LANES), 1)
    odd = jnp.where(lane >= TILE, 1, 0)
    entry = lane - odd * TILE

    def pack(slot, store):
        rest = jnp.zeros((GROUP, LANES), jnp.float32)
        for j in range(packed_tiles):
            upper = raw[slot, :, j * LANES:(j + 1) * LANES].astype(jnp.float32)
            start = (packed_tiles + j) * LANES
            lower = raw[slot, :, start:start + LANES].astype(jnp.float32)
            row = odd + 2 * j
            both = jnp.where(entry >= row, upper, pltpu.roll(lower, ROLL, 1))
            store(j, both.astype(jnp.bfloat16))
            rest = jnp.where(entry == row + HALF, lower, rest)
        return rest

    def r_copy(there, here):
        return pltpu.make_async_remote_copy(
            src_ref=rest_out.at[there], dst_ref=rest_in.at[pl.ds(here * GROUP, GROUP)],
            send_sem=r_send.at[there], recv_sem=r_recv.at[here],
            device_id={"col": there}, device_id_type=MESH,
        )

    for v in range(pairs):

        def outgoing(step, carry):
            n = v * n_col + step

            @pl.when(n + AHEAD - 1 < steps)
            def _():
                load(n + AHEAD - 1).start()

            load(n).wait()
            there = target(step)

            def store(j, value):
                send[there, v, :, j * LANES:(j + 1) * LANES] = value

            rest = pack(lax.rem(n, AHEAD), store)
            if v == 0:
                rest_sum[there] = rest

                @pl.when(step < n_col - 1)
                def _():
                    c_copy(v, there, me).start()
            else:
                rest_sum[there] += pltpu.roll(rest, v * HALF, 1)
            return carry

        lax.fori_loop(0, n_col, outgoing, 0)

    rest_out[...] = rest_sum[...].astype(jnp.bfloat16)

    def rests(step, carry):
        r_copy(target(step), me).start()
        return carry

    lax.fori_loop(0, n_col - 1, rests, 0)
    for v in range(1, pairs):

        def later(step, carry):
            c_copy(v, target(step), me).start()
            return carry

        lax.fori_loop(0, n_col - 1, later, 0)
    my_rows = pl.ds(pl.multiple_of(me * GROUP, GROUP), GROUP)
    for v in range(pairs):
        recv[v, my_rows, :] = send[me, v]
    rest_in[my_rows, :] = rest_out[me]

    half = lax.broadcasted_iota(jnp.int32, (width, LANES), 1) < TILE
    x_copy.wait()
    for j in range(x_raw.shape[1] // LANES):
        a = x_raw[:, j * LANES:(j + 1) * LANES]
        b = pltpu.roll(a, TILE, 1)
        for k, value in enumerate((jnp.where(half, a, b), jnp.where(half, b, a))):
            high, low = split(value)
            x_ref[2 * j + k, :, :LANES] = high
            x_ref[2 * j + k, :, LANES:] = low
    z_copy.wait()

    def parts_of(t, carry):
        high, low = split(z_raw[pl.ds(pl.multiple_of(t * TILE, TILE), TILE), :])
        z_ref[t, :TILE] = high
        z_ref[t, TILE:] = low
        return carry

    lax.fori_loop(0, z_ref.shape[0], parts_of, 0)

    slab_half = lax.broadcasted_iota(jnp.int32, (s_dev, LANES), 1) < TILE

    def expand(r):
        for j in range(TILE * TILE // LANES):
            a = s_raw[r, :, j * LANES:(j + 1) * LANES].astype(jnp.float32)
            b = pltpu.roll(a, TILE, 1)
            slab[pl.ds(r * s_dev * TILE + 2 * j, s_dev, stride=TILE), :] = jnp.where(slab_half, a, b)
            slab[pl.ds(r * s_dev * TILE + 2 * j + 1, s_dev, stride=TILE), :] = jnp.where(slab_half, b, a)

    s_copy.wait()
    expand(own)

    wide = lax.broadcasted_iota(jnp.int32, (TILE, LANES), 1)
    first = wide < TILE
    e = lax.broadcasted_iota(jnp.int32, (HALF, LANES), 0)
    f = lax.broadcasted_iota(jnp.int32, (HALF, LANES), 1)
    f = jnp.where(f >= TILE, f - TILE, f)

    def terms(i, t):
        square = slab[pl.ds(pl.multiple_of(i * TILE, TILE), TILE), :].astype(jnp.bfloat16)
        panel = jnp.dot(square, z_ref[t], preferred_element_type=jnp.float32)
        high, low = split(panel)
        right = jnp.concatenate([high, low, high, low], axis=0)
        done = []
        for v in range(pairs):
            cut = slice(v * LANES, (v + 1) * LANES)
            term = jnp.dot(x_ref[t, cut], right[:, cut], preferred_element_type=jnp.float32)
            term = jnp.where(first, term[:TILE], term[TILE:])
            done.append(term.astype(jnp.bfloat16).astype(jnp.float32))
        if pairs % 2:
            done.append(done[-1])
        for v in range(0, len(done), 2):
            turned = jnp.concatenate(done[v:v + 2], axis=0).T
            crossed = pltpu.roll(turned, TILE, 1)
            done[v] += jnp.where(first, turned[:TILE], crossed[TILE:])
            done[v + 1] += jnp.where(first, crossed[:TILE], turned[TILE:])
        for v in range(pairs):
            upper, lower = done[v][:HALF], done[v][HALF:]
            both = jnp.where(f > e, upper, jnp.where(f < e, pltpu.roll(lower, ROLL, 1), 0.5 * upper))
            folded[pl.ds(pl.multiple_of((v * rows + i) * HALF, HALF), HALF), :] = both
            rest = jnp.sum(jnp.where(f == e + HALF, 0.5 * lower, 0.0), axis=0, keepdims=True)
            corner[pl.ds(v * rows + i, 1), :] = rest

    def first_rows(n, carry):
        for k in range(TOGETHER):
            inner = n * TOGETHER + k
            terms(own * s_dev + inner, own_tile[0, inner])
        return carry

    lax.fori_loop(0, s_dev // TOGETHER, first_rows, 0)
    for there in mates:
        tile_copy(there, there).wait_recv()
        slab_copy(there, there).wait_recv()
        expand(there)
    tile_in[own] = tile_out[...]
    tile_move = pltpu.make_async_copy(tile_in, tile_all, in_sem.at[3])
    tile_move.start()
    tile_move.wait()

    def other_rows(n, carry):
        for k in range(TOGETHER):
            at = n * TOGETHER + k
            there = lax.rem(own + lax.div(at, s_dev), n_row)
            inner = lax.rem(at, s_dev)
            terms(there * s_dev + inner, tile_all[there, 0, inner])
        return carry

    lax.fori_loop(s_dev // TOGETHER, rows // TOGETHER, other_rows, 0)

    spot = lax.broadcasted_iota(jnp.int32, (LANES, LANES), 1)
    near = spot < TILE
    parity = jnp.where(near, 0, 1) == lax.rem(spot, 2)
    for v in range(pairs):

        def lay(chunk, carry):
            base = (v * rows + chunk * LANES) * HALF
            for j in range(packed_tiles + 1):
                if j < packed_tiles:
                    a = folded[pl.ds(base + 2 * j, LANES, stride=HALF), :]
                    b = folded[pl.ds(base + 2 * j + 1, LANES, stride=HALF), :]
                else:
                    a = b = corner[pl.ds(pl.multiple_of(v * rows + chunk * LANES, LANES), LANES), :]
                u0 = jnp.where(near, a, pltpu.roll(b, TILE, 1))
                u1 = jnp.where(near, pltpu.roll(a, TILE, 1), b)
                if j == packed_tiles:
                    u0 = jnp.where(parity, u0, 0.0)
                    u1 = jnp.where(parity, u1, 0.0)
                    if v:
                        u0 = pltpu.roll(u0, v * HALF, 1)
                        u1 = pltpu.roll(u1, v * HALF, 1)
                parts = split(u0) + split(u1)
                for k, value in enumerate(parts):
                    at = pl.multiple_of(k * rows + chunk * LANES, LANES)
                    left[v, pl.ds(at, LANES), j * LANES:(j + 1) * LANES] = value
            return carry

        lax.fori_loop(0, rows // LANES, lay, 0)

    perm_copy.wait()
    keep = GROUP // 2
    group = lax.div(lax.broadcasted_iota(jnp.int32, (1, LANES), 1), keep)
    for r in range(n_row):
        for v in range(pairs):
            for h in range(across // LANES):
                value = jnp.zeros((1, LANES), jnp.int32)
                for g in range(LANES // keep):
                    start = ((r * pairs + v) * 2 + g % 2) * (across // 2)
                    old = (h * (LANES // GROUP) + g // 2) * keep
                    turn = (g * keep - old) % LANES
                    piece = perm_raw[:, start:start + LANES]
                    piece = pltpu.roll(piece, turn, 1) if turn else piece
                    value = jnp.where(group == g, piece, value)
                perm_ref[r, v, :, h * LANES:(h + 1) * LANES] = value

    column = lax.broadcasted_iota(jnp.int32, (LANES, across), 0)
    for r in range(n_row):
        for v in range(pairs):

            def mark(n, carry):
                start = pl.multiple_of(n * LANES, LANES)
                value = jnp.where(column + n * LANES == perm_ref[r, v], 1.0, 0.0)
                hot[r, v, pl.ds(start, LANES), :] = value.astype(jnp.bfloat16)
                return carry

            lax.fori_loop(0, columns // LANES, mark, 0)

    even = lax.rem(lax.broadcasted_iota(jnp.int32, (rows, across), 1), GROUP) < GROUP // 2

    def place(v, r, fresh):
        high, low = split(theirs[v, r])
        value = jnp.concatenate([high, low], axis=0)
        value = lax.dot_general(value, hot[r, v], NT, preferred_element_type=jnp.float32)
        value = value[:s_dev] + value[s_dev:]
        total[...] = value if fresh else total[...] + value

    def place_mates(v):
        for there in mates:
            y_copy(v, there, there).wait_recv()
            place(v, there, False)

    for v in range(pairs):
        if v > 0:
            place_mates(v - 1)

        def landed(n, carry):
            there = target(n)
            c_copy(v, there, there).wait_recv()
            if v == 0:
                r_copy(there, there).wait_recv()
            return carry

        lax.fori_loop(0, n_col - 1, landed, 0)
        most = packed_tiles * LANES
        both = lax.dot_general(left[v, :, :most], recv[v], NT, preferred_element_type=jnp.float32)
        both += lax.dot_general(left[v, :, most:], rest_in[...], NT, preferred_element_type=jnp.float32)
        u0 = both[:rows] + both[rows:2 * rows]
        u1 = both[2 * rows:3 * rows] + both[3 * rows:]
        value = jnp.where(even, u0, u1)
        for block in range(rows // RB):
            q, r = divmod(block, n_row)
            mine[v, r, q * RB:(q + 1) * RB, :] = value[block * RB:(block + 1) * RB]
        for there in mates:
            y_copy(v, there, own).start()
        theirs[v, own] = mine[v, own]
        place(v, own, v == 0)
        if v == pairs - 1:
            place_mates(v)

    out_cols = columns // n_col
    for c in range(n_col):
        placed[c] = total[:, c * out_cols:(c + 1) * out_cols]

    near_ones = [lax.rem(my_place + k, half_col) for k in range(1, half_col)]
    for which in range(2):
        for there in near_ones:
            p_copy(which, there, my_place).start()
    summed = placed[far_side * half_col + my_place]
    for there in near_ones:
        p_copy(0, there, there).wait_recv()
        summed = summed + arrived[0, there]
    over_out[...] = summed
    over_copy.start()
    summed = placed[me]
    for there in near_ones:
        p_copy(1, there, there).wait_recv()
        summed = summed + arrived[1, there]
    over_copy.wait_recv()
    out_ref[...] = summed + over_in[...]
    over_copy.wait_send()
    for which in range(2):
        for there in near_ones:
            p_copy(which, there, my_place).wait_send()

    def done(n, carry):
        there = target(n)
        for v in range(pairs):
            c_copy(v, there, me).wait_send()
        r_copy(there, me).wait_send()
        return carry

    lax.fori_loop(0, n_col - 1, done, 0)
    for there in mates:
        tile_copy(there, own).wait_send()
        slab_copy(there, own).wait_send()
        for v in range(pairs):
            y_copy(v, there, own).wait_send()


def body(n_row, n_col, primal, dual_inv, col_values, col_perm, slab_values, slab_tile):
    tile_count = col_values.shape[1]
    order = primal.shape[1]
    columns = col_perm.shape[1]
    s_dev = slab_values.shape[1]
    rows = n_row * s_dev
    keep = col_values.shape[2]
    part = tile_count // n_row
    width = part * TILE
    pairs = part // 2
    col = col_values.reshape(n_col, tile_count // 2, GROUP, TILE * TILE)

    packed = TILE * TILE // 2 + LANES
    out_cols = columns // n_col
    across = n_col * GROUP
    vmem = pl.BlockSpec(memory_space=pltpu.VMEM)
    whole = pl.BlockSpec(memory_space=pl.ANY)
    dma = pltpu.SemaphoreType.DMA
    f32, bf16, i32 = jnp.float32, jnp.bfloat16, jnp.int32
    return pl.pallas_call(
        functools.partial(kernel, n_row, n_col),
        out_shape=jax.ShapeDtypeStruct((s_dev, out_cols), f32),
        in_specs=[pl.BlockSpec(memory_space=pltpu.SMEM), vmem, whole, whole, whole, whole, whole],
        out_specs=vmem,
        scratch_shapes=[
            pltpu.VMEM((width, order), f32),
            pltpu.VMEM((order, width), f32),
            pltpu.VMEM((order // TILE, width, 2 * LANES), bf16),
            pltpu.VMEM((order // TILE, 2 * TILE, width), bf16),
            pltpu.VMEM((8, LANES), i32),
            pltpu.VMEM((n_row, 8, LANES), i32),
            pltpu.SMEM((n_row, 8, LANES), i32),
            pltpu.VMEM((n_row, s_dev, TILE * TILE), bf16),
            pltpu.VMEM((rows * TILE, LANES), f32),
            pltpu.VMEM((AHEAD, GROUP, TILE * TILE), bf16),
            pltpu.VMEM((n_col, pairs, GROUP, packed - LANES), bf16),
            pltpu.VMEM((pairs, across, packed - LANES), bf16),
            pltpu.VMEM((pairs * rows * HALF, LANES), f32),
            pltpu.VMEM((pairs * rows, LANES), f32),
            pltpu.VMEM((pairs, 4 * rows, packed), bf16),
            pltpu.VMEM((pairs, n_row, s_dev, across), f32),
            pltpu.VMEM((pairs, n_row, s_dev, across), f32),
            pltpu.VMEM((n_row, pairs, columns, across), bf16),
            pltpu.VMEM((s_dev, columns), f32),
            pltpu.VMEM((n_col, s_dev, out_cols), f32),
            pltpu.VMEM((2, n_col // 2, s_dev, out_cols), f32),
            pltpu.VMEM((s_dev, out_cols), f32),
            pltpu.VMEM((s_dev, out_cols), f32),
            pltpu.VMEM((n_col, GROUP, LANES), f32),
            pltpu.VMEM((n_col, GROUP, LANES), bf16),
            pltpu.VMEM((across, LANES), bf16),
            pltpu.VMEM((1, columns), i32),
            pltpu.VMEM((n_row, pairs, 1, across), i32),
            dma((AHEAD,)), dma((5,)), dma((pairs, n_col)), dma((pairs, n_col)),
            dma((n_row,)), dma((n_row,)), dma((n_row,)), dma((n_row,)),
            dma((pairs, n_row)), dma((pairs, n_row)), dma((2, n_col // 2)), dma((2, n_col // 2)),
            dma((1,)), dma((1,)), dma((n_col,)), dma((n_col,)),
        ],
        compiler_params=pltpu.CompilerParams(
            collective_id=0, has_side_effects=True, vmem_limit_bytes=60 * 1024 * 1024
        ),
    )(slab_tile, slab_tile, col_perm, primal, dual_inv, slab_values, col)


def solution(mesh):
    def run(*args):
        return body(mesh.shape["row"], mesh.shape["col"], *args)

    return jax.shard_map(
        run,
        mesh=mesh,
        in_specs=(
            P("col", None, None),
            P("col", None, None),
            P(None, None, "col", None),
            P(),
            P("col", "row", None),
            P("col", "row"),
        ),
        out_specs=P("row", "col"),
        check_vma=False,
    )
```

```python
import functools

import jax
import jax.numpy as jnp
from jax import lax
from jax.experimental import pallas as pl
from jax.experimental.pallas import tpu as pltpu
from jax.sharding import PartitionSpec as P

TILE = 64
HALF = TILE // 2
RB = 32
LANES = 128
GROUP = 16
ROLL = LANES - HALF
TOGETHER = 4
AHEAD = 16
MESH = pl.DeviceIdType.MESH
NT = (((1,), (1,)), ((), ()))


def split(value):
    high = value.astype(jnp.bfloat16)
    low = (value - high.astype(jnp.float32)).astype(jnp.bfloat16)
    return high, low


def kernel(
    n_row, n_col, own_tile, tile_ref, perm_hbm, x_hbm, z_hbm, s_hbm, col_ref, out_ref,
    x_raw, z_raw, x_ref, z_ref, tile_out, tile_in, tile_all, s_raw, slab,
    raw, send, recv, folded, corner, left, mine, theirs, hot, total, placed, arrived, over_out, over_in,
    rest_sum, rest_out, rest_in, perm_raw, perm_ref,
    load_sem, in_sem, c_send, c_recv, s_send, s_recv, t_send, t_recv, y_send, y_recv, p_send, p_recv, o_send, o_recv, r_send, r_recv,
):
    me = lax.axis_index("col")
    own = lax.axis_index("row")
    s_dev = s_hbm.shape[1]
    rows = n_row * s_dev
    pairs = send.shape[1]
    width = pairs * LANES
    packed_tiles = TILE * TILE // 2 // LANES
    across = n_col * GROUP
    columns = hot.shape[2]

    x_copy = pltpu.make_async_copy(x_hbm.at[0, pl.ds(own * width, width)], x_raw, in_sem.at[0])
    z_copy = pltpu.make_async_copy(
        z_hbm.at[0, :, pl.ds(pl.multiple_of(own * width, LANES), width)], z_raw, in_sem.at[1]
    )
    s_copy = pltpu.make_async_copy(s_hbm.at[0], s_raw.at[own], in_sem.at[2])
    perm_copy = pltpu.make_async_copy(perm_hbm.at[pl.ds(me, 1)], perm_raw, in_sem.at[4])

    def target(n):
        side = lax.rem(lax.div(me, n_col // 2) + 1 + lax.div(n, n_col // 2), 2)
        return side * (n_col // 2) + lax.rem(me + 1 + n, n_col // 2)

    def load(n):
        slot = lax.rem(n, AHEAD)
        return pltpu.make_async_copy(
            col_ref.at[target(lax.rem(n, n_col)), own * pairs + lax.div(n, n_col)],
            raw.at[slot], load_sem.at[slot],
        )

    steps = pairs * n_col
    for n in range(min(AHEAD - 1, steps)):
        load(n).start()
    x_copy.start()
    z_copy.start()
    s_copy.start()
    perm_copy.start()

    barrier = pltpu.get_barrier_semaphore()
    for k in range(1, n_col):
        pl.semaphore_signal(barrier, inc=1, device_id={"col": lax.rem(me + k, n_col)}, device_id_type=MESH)
    for k in range(1, n_row):
        pl.semaphore_signal(barrier, inc=1, device_id={"row": lax.rem(own + k, n_row)}, device_id_type=MESH)

    tile_out[...] = jnp.zeros_like(tile_out)
    tile_out[0:1, 0:s_dev] = tile_ref[...]
    pl.semaphore_wait(barrier, n_col + n_row - 2)

    def row_copy(src, dst, out_sem, in_sem, there):
        return pltpu.make_async_remote_copy(
            src_ref=src, dst_ref=dst, send_sem=out_sem, recv_sem=in_sem,
            device_id={"row": there}, device_id_type=MESH,
        )

    def tile_copy(there, here):
        return row_copy(tile_out, tile_in.at[here], t_send.at[there], t_recv.at[here], there)

    def slab_copy(there, here):
        return row_copy(s_hbm.at[0], s_raw.at[here], s_send.at[there], s_recv.at[here], there)

    def y_copy(v, there, here):
        return row_copy(
            mine.at[v, there], theirs.at[v, here], y_send.at[v, there], y_recv.at[v, here], there
        )

    def c_copy(v, there, here):
        return pltpu.make_async_remote_copy(
            src_ref=send.at[there, v], dst_ref=recv.at[v, pl.ds(here * GROUP, GROUP)],
            send_sem=c_send.at[v, there], recv_sem=c_recv.at[v, here],
            device_id={"col": there}, device_id_type=MESH,
        )

    half_col = n_col // 2
    my_side = lax.div(me, half_col)
    my_place = lax.rem(me, half_col)
    far_side = 1 - my_side
    sides = (far_side, my_side)

    def p_copy(which, there, here):
        return pltpu.make_async_remote_copy(
            src_ref=placed.at[sides[which] * half_col + there], dst_ref=arrived.at[which, here],
            send_sem=p_send.at[which, there], recv_sem=p_recv.at[which, here],
            device_id={"col": my_side * half_col + there}, device_id_type=MESH,
        )

    over_copy = pltpu.make_async_remote_copy(
        src_ref=over_out, dst_ref=over_in, send_sem=o_send.at[0], recv_sem=o_recv.at[0],
        device_id={"col": far_side * half_col + my_place}, device_id_type=MESH,
    )

    mates = [lax.rem(own + k, n_row) for k in range(1, n_row)]
    for there in mates:
        tile_copy(there, own).start()
        slab_copy(there, own).start()

    lane = lax.broadcasted_iota(jnp.int32, (GROUP, LANES), 1)
    odd = jnp.where(lane >= TILE, 1, 0)
    entry = lane - odd * TILE

    def pack(slot, store):
        rest = jnp.zeros((GROUP, LANES), jnp.float32)
        for j in range(packed_tiles):
            upper = raw[slot, :, j * LANES:(j + 1) * LANES].astype(jnp.float32)
            start = (packed_tiles + j) * LANES
            lower = raw[slot, :, start:start + LANES].astype(jnp.float32)
            row = odd + 2 * j
            both = jnp.where(entry >= row, upper, pltpu.roll(lower, ROLL, 1))
            store(j, both.astype(jnp.bfloat16))
            rest = jnp.where(entry == row + HALF, lower, rest)
        return rest

    def r_copy(there, here):
        return pltpu.make_async_remote_copy(
            src_ref=rest_out.at[there], dst_ref=rest_in.at[pl.ds(here * GROUP, GROUP)],
            send_sem=r_send.at[there], recv_sem=r_recv.at[here],
            device_id={"col": there}, device_id_type=MESH,
        )

    for v in range(pairs):

        def outgoing(step, carry):
            n = v * n_col + step

            @pl.when(n + AHEAD - 1 < steps)
            def _():
                load(n + AHEAD - 1).start()

            load(n).wait()
            there = target(step)

            def store(j, value):
                send[there, v, :, j * LANES:(j + 1) * LANES] = value

            rest = pack(lax.rem(n, AHEAD), store)
            if v == 0:
                rest_sum[there] = rest

                @pl.when(step < n_col - 1)
                def _():
                    c_copy(v, there, me).start()
            else:
                rest_sum[there] += pltpu.roll(rest, v * HALF, 1)
            return carry

        lax.fori_loop(0, n_col, outgoing, 0)

    rest_out[...] = rest_sum[...].astype(jnp.bfloat16)

    def rests(step, carry):
        r_copy(target(step), me).start()
        return carry

    lax.fori_loop(0, n_col - 1, rests, 0)
    for v in range(1, pairs):

        def later(step, carry):
            c_copy(v, target(step), me).start()
            return carry

        lax.fori_loop(0, n_col - 1, later, 0)
    my_rows = pl.ds(pl.multiple_of(me * GROUP, GROUP), GROUP)
    for v in range(pairs):
        recv[v, my_rows, :] = send[me, v]
    rest_in[my_rows, :] = rest_out[me]

    half = lax.broadcasted_iota(jnp.int32, (width, LANES), 1) < TILE
    x_copy.wait()
    for j in range(x_raw.shape[1] // LANES):
        a = x_raw[:, j * LANES:(j + 1) * LANES]
        b = pltpu.roll(a, TILE, 1)
        for k, value in enumerate((jnp.where(half, a, b), jnp.where(half, b, a))):
            high, low = split(value)
            x_ref[2 * j + k, :, :LANES] = high
            x_ref[2 * j + k, :, LANES:] = low
    z_copy.wait()

    def parts_of(t, carry):
        high, low = split(z_raw[pl.ds(pl.multiple_of(t * TILE, TILE), TILE), :])
        z_ref[t, :TILE] = high
        z_ref[t, TILE:] = low
        return carry

    lax.fori_loop(0, z_ref.shape[0], parts_of, 0)

    slab_half = lax.broadcasted_iota(jnp.int32, (s_dev, LANES), 1) < TILE

    def expand(r):
        for j in range(TILE * TILE // LANES):
            a = s_raw[r, :, j * LANES:(j + 1) * LANES].astype(jnp.float32)
            b = pltpu.roll(a, TILE, 1)
            slab[pl.ds(r * s_dev * TILE + 2 * j, s_dev, stride=TILE), :] = jnp.where(slab_half, a, b)
            slab[pl.ds(r * s_dev * TILE + 2 * j + 1, s_dev, stride=TILE), :] = jnp.where(slab_half, b, a)

    s_copy.wait()
    expand(own)

    wide = lax.broadcasted_iota(jnp.int32, (TILE, LANES), 1)
    first = wide < TILE
    e = lax.broadcasted_iota(jnp.int32, (HALF, LANES), 0)
    f = lax.broadcasted_iota(jnp.int32, (HALF, LANES), 1)
    f = jnp.where(f >= TILE, f - TILE, f)

    def terms(i, t):
        square = slab[pl.ds(pl.multiple_of(i * TILE, TILE), TILE), :].astype(jnp.bfloat16)
        panel = jnp.dot(square, z_ref[t], preferred_element_type=jnp.float32)
        high, low = split(panel)
        right = jnp.concatenate([high, low, high, low], axis=0)
        done = []
        for v in range(pairs):
            cut = slice(v * LANES, (v + 1) * LANES)
            term = jnp.dot(x_ref[t, cut], right[:, cut], preferred_element_type=jnp.float32)
            term = jnp.where(first, term[:TILE], term[TILE:])
            done.append(term.astype(jnp.bfloat16).astype(jnp.float32))
        if pairs % 2:
            done.append(done[-1])
        for v in range(0, len(done), 2):
            turned = jnp.concatenate(done[v:v + 2], axis=0).T
            crossed = pltpu.roll(turned, TILE, 1)
            done[v] += jnp.where(first, turned[:TILE], crossed[TILE:])
            done[v + 1] += jnp.where(first, crossed[:TILE], turned[TILE:])
        for v in range(pairs):
            upper, lower = done[v][:HALF], done[v][HALF:]
            both = jnp.where(f > e, upper, jnp.where(f < e, pltpu.roll(lower, ROLL, 1), 0.5 * upper))
            folded[pl.ds(pl.multiple_of((v * rows + i) * HALF, HALF), HALF), :] = both
            rest = jnp.sum(jnp.where(f == e + HALF, 0.5 * lower, 0.0), axis=0, keepdims=True)
            corner[pl.ds(v * rows + i, 1), :] = rest

    def first_rows(n, carry):
        for k in range(TOGETHER):
            inner = n * TOGETHER + k
            terms(own * s_dev + inner, own_tile[0, inner])
        return carry

    lax.fori_loop(0, s_dev // TOGETHER, first_rows, 0)
    for there in mates:
        tile_copy(there, there).wait_recv()
        slab_copy(there, there).wait_recv()
        expand(there)
    tile_in[own] = tile_out[...]
    tile_move = pltpu.make_async_copy(tile_in, tile_all, in_sem.at[3])
    tile_move.start()
    tile_move.wait()

    def other_rows(n, carry):
        for k in range(TOGETHER):
            at = n * TOGETHER + k
            there = lax.rem(own + lax.div(at, s_dev), n_row)
            inner = lax.rem(at, s_dev)
            terms(there * s_dev + inner, tile_all[there, 0, inner])
        return carry

    lax.fori_loop(s_dev // TOGETHER, rows // TOGETHER, other_rows, 0)

    spot = lax.broadcasted_iota(jnp.int32, (LANES, LANES), 1)
    near = spot < TILE
    parity = jnp.where(near, 0, 1) == lax.rem(spot, 2)
    for v in range(pairs):

        def lay(chunk, carry):
            base = (v * rows + chunk * LANES) * HALF
            for j in range(packed_tiles + 1):
                if j < packed_tiles:
                    a = folded[pl.ds(base + 2 * j, LANES, stride=HALF), :]
                    b = folded[pl.ds(base + 2 * j + 1, LANES, stride=HALF), :]
                else:
                    a = b = corner[pl.ds(pl.multiple_of(v * rows + chunk * LANES, LANES), LANES), :]
                u0 = jnp.where(near, a, pltpu.roll(b, TILE, 1))
                u1 = jnp.where(near, pltpu.roll(a, TILE, 1), b)
                if j == packed_tiles:
                    u0 = jnp.where(parity, u0, 0.0)
                    u1 = jnp.where(parity, u1, 0.0)
                    if v:
                        u0 = pltpu.roll(u0, v * HALF, 1)
                        u1 = pltpu.roll(u1, v * HALF, 1)
                parts = split(u0) + split(u1)
                for k, value in enumerate(parts):
                    at = pl.multiple_of(k * rows + chunk * LANES, LANES)
                    left[v, pl.ds(at, LANES), j * LANES:(j + 1) * LANES] = value
            return carry

        lax.fori_loop(0, rows // LANES, lay, 0)

    perm_copy.wait()
    keep = GROUP // 2
    group = lax.div(lax.broadcasted_iota(jnp.int32, (1, LANES), 1), keep)
    for r in range(n_row):
        for v in range(pairs):
            for h in range(across // LANES):
                value = jnp.zeros((1, LANES), jnp.int32)
                for g in range(LANES // keep):
                    start = ((r * pairs + v) * 2 + g % 2) * (across // 2)
                    old = (h * (LANES // GROUP) + g // 2) * keep
                    turn = (g * keep - old) % LANES
                    piece = perm_raw[:, start:start + LANES]
                    piece = pltpu.roll(piece, turn, 1) if turn else piece
                    value = jnp.where(group == g, piece, value)
                perm_ref[r, v, :, h * LANES:(h + 1) * LANES] = value

    column = lax.broadcasted_iota(jnp.int32, (LANES, across), 0)
    for r in range(n_row):
        for v in range(pairs):

            def mark(n, carry):
                start = pl.multiple_of(n * LANES, LANES)
                value = jnp.where(column + n * LANES == perm_ref[r, v], 1.0, 0.0)
                hot[r, v, pl.ds(start, LANES), :] = value.astype(jnp.bfloat16)
                return carry

            lax.fori_loop(0, columns // LANES, mark, 0)

    even = lax.rem(lax.broadcasted_iota(jnp.int32, (rows, across), 1), GROUP) < GROUP // 2

    def place(v, r, fresh):
        high, low = split(theirs[v, r])
        value = jnp.concatenate([high, low], axis=0)
        value = lax.dot_general(value, hot[r, v], NT, preferred_element_type=jnp.float32)
        value = value[:s_dev] + value[s_dev:]
        total[...] = value if fresh else total[...] + value

    def place_mates(v):
        for there in mates:
            y_copy(v, there, there).wait_recv()
            place(v, there, False)

    for v in range(pairs):
        if v > 0:
            place_mates(v - 1)

        def landed(n, carry):
            there = target(n)
            c_copy(v, there, there).wait_recv()
            if v == 0:
                r_copy(there, there).wait_recv()
            return carry

        lax.fori_loop(0, n_col - 1, landed, 0)
        most = packed_tiles * LANES
        both = lax.dot_general(left[v, :, :most], recv[v], NT, preferred_element_type=jnp.float32)
        both += lax.dot_general(left[v, :, most:], rest_in[...], NT, preferred_element_type=jnp.float32)
        u0 = both[:rows] + both[rows:2 * rows]
        u1 = both[2 * rows:3 * rows] + both[3 * rows:]
        value = jnp.where(even, u0, u1)
        for block in range(rows // RB):
            q, r = divmod(block, n_row)
            mine[v, r, q * RB:(q + 1) * RB, :] = value[block * RB:(block + 1) * RB]
        for there in mates:
            y_copy(v, there, own).start()
        theirs[v, own] = mine[v, own]
        place(v, own, v == 0)
        if v == pairs - 1:
            place_mates(v)

    out_cols = columns // n_col
    for c in range(n_col):
        placed[c] = total[:, c * out_cols:(c + 1) * out_cols]

    near_ones = [lax.rem(my_place + k, half_col) for k in range(1, half_col)]
    for which in range(2):
        for there in near_ones:
            p_copy(which, there, my_place).start()
    summed = placed[far_side * half_col + my_place]
    for there in near_ones:
        p_copy(0, there, there).wait_recv()
        summed = summed + arrived[0, there]
    over_out[...] = summed
    over_copy.start()
    summed = placed[me]
    for there in near_ones:
        p_copy(1, there, there).wait_recv()
        summed = summed + arrived[1, there]
    over_copy.wait_recv()
    out_ref[...] = summed + over_in[...]
    over_copy.wait_send()
    for which in range(2):
        for there in near_ones:
            p_copy(which, there, my_place).wait_send()

    def done(n, carry):
        there = target(n)
        for v in range(pairs):
            c_copy(v, there, me).wait_send()
        r_copy(there, me).wait_send()
        return carry

    lax.fori_loop(0, n_col - 1, done, 0)
    for there in mates:
        tile_copy(there, own).wait_send()
        slab_copy(there, own).wait_send()
        for v in range(pairs):
            y_copy(v, there, own).wait_send()


def body(n_row, n_col, primal, dual_inv, col_values, col_perm, slab_values, slab_tile):
    tile_count = col_values.shape[1]
    order = primal.shape[1]
    columns = col_perm.shape[1]
    s_dev = slab_values.shape[1]
    rows = n_row * s_dev
    keep = col_values.shape[2]
    part = tile_count // n_row
    width = part * TILE
    pairs = part // 2
    col = col_values.reshape(n_col, tile_count // 2, GROUP, TILE * TILE)

    packed = TILE * TILE // 2 + LANES
    out_cols = columns // n_col
    across = n_col * GROUP
    vmem = pl.BlockSpec(memory_space=pltpu.VMEM)
    whole = pl.BlockSpec(memory_space=pl.ANY)
    dma = pltpu.SemaphoreType.DMA
    f32, bf16, i32 = jnp.float32, jnp.bfloat16, jnp.int32
    return pl.pallas_call(
        functools.partial(kernel, n_row, n_col),
        out_shape=jax.ShapeDtypeStruct((s_dev, out_cols), f32),
        in_specs=[pl.BlockSpec(memory_space=pltpu.SMEM), vmem, whole, whole, whole, whole, whole],
        out_specs=vmem,
        scratch_shapes=[
            pltpu.VMEM((width, order), f32),
            pltpu.VMEM((order, width), f32),
            pltpu.VMEM((order // TILE, width, 2 * LANES), bf16),
            pltpu.VMEM((order // TILE, 2 * TILE, width), bf16),
            pltpu.VMEM((8, LANES), i32),
            pltpu.VMEM((n_row, 8, LANES), i32),
            pltpu.SMEM((n_row, 8, LANES), i32),
            pltpu.VMEM((n_row, s_dev, TILE * TILE), bf16),
            pltpu.VMEM((rows * TILE, LANES), f32),
            pltpu.VMEM((AHEAD, GROUP, TILE * TILE), bf16),
            pltpu.VMEM((n_col, pairs, GROUP, packed - LANES), bf16),
            pltpu.VMEM((pairs, across, packed - LANES), bf16),
            pltpu.VMEM((pairs * rows * HALF, LANES), f32),
            pltpu.VMEM((pairs * rows, LANES), f32),
            pltpu.VMEM((pairs, 4 * rows, packed), bf16),
            pltpu.VMEM((pairs, n_row, s_dev, across), f32),
            pltpu.VMEM((pairs, n_row, s_dev, across), f32),
            pltpu.VMEM((n_row, pairs, columns, across), bf16),
            pltpu.VMEM((s_dev, columns), f32),
            pltpu.VMEM((n_col, s_dev, out_cols), f32),
            pltpu.VMEM((2, n_col // 2, s_dev, out_cols), f32),
            pltpu.VMEM((s_dev, out_cols), f32),
            pltpu.VMEM((s_dev, out_cols), f32),
            pltpu.VMEM((n_col, GROUP, LANES), f32),
            pltpu.VMEM((n_col, GROUP, LANES), bf16),
            pltpu.VMEM((across, LANES), bf16),
            pltpu.VMEM((1, columns), i32),
            pltpu.VMEM((n_row, pairs, 1, across), i32),
            dma((AHEAD,)), dma((5,)), dma((pairs, n_col)), dma((pairs, n_col)),
            dma((n_row,)), dma((n_row,)), dma((n_row,)), dma((n_row,)),
            dma((pairs, n_row)), dma((pairs, n_row)), dma((2, n_col // 2)), dma((2, n_col // 2)),
            dma((1,)), dma((1,)), dma((n_col,)), dma((n_col,)),
        ],
        compiler_params=pltpu.CompilerParams(
            collective_id=0, has_side_effects=True, vmem_limit_bytes=60 * 1024 * 1024
        ),
    )(slab_tile, slab_tile, col_perm, primal, dual_inv, slab_values, col)


def solution(mesh):
    def run(*args):
        return body(mesh.shape["row"], mesh.shape["col"], *args)

    return jax.shard_map(
        run,
        mesh=mesh,
        in_specs=(
            P("col", None, None),
            P("col", None, None),
            P(None, None, "col", None),
            P(),
            P("col", "row", None),
            P("col", "row"),
        ),
        out_specs=P("row", "col"),
        check_vma=False,
    )
```
